32 devices in a mesh: group: 2 (over y), gene: 4 (over z), lat: 2 (over x), sub: 2 (over core).
Axes of the slice: x: 2, y: 2, z: 4, core: 2. Of those that a mesh axis runs over, the one named last changes fastest.
Arguments:
- cell_index: int32 [2048], P(('group', 'lat', 'sub')), parts along dimension 0, may hold values from 0 to 511
- coords_table: float32 [4, 2048], P('group', ('lat', 'sub')), parts along dimension 0, may hold values from 0 to 1
- expr_table: bfloat16 [4096, 16384], P(('group', 'lat', 'sub'), 'gene'), parts along dimension 0, may hold values from -6 to 6
- inducing: float32 [4, 64, 8192], P('group', 'lat', 'sub'), parts along dimension 0, may hold values from 0 to 1
- ind_weights: float32 [128, 8192], P(('group', 'lat'), 'sub'), parts along dimension 0, may hold values from -0.6 to 0.6
- lengthscale: float32 [128], P(('group', 'lat')), parts along dimension 0, may hold values from 0.02 to 0.1
- variance: float32 [128], P(('group', 'lat')), parts along dimension 0, may hold values from 0.5 to 2
- mixing: bfloat16 [128, 16384], P('group', 'gene'), parts along dimension 0, may hold values from -0.75 to 0.75
- noise_prec: float32 [32768], P(('group', 'gene')), parts along dimension 0, may hold values from 0.5 to 4
Outputs:
- grad_mixing: float32 [128, 16384], P('group', 'gene'), parts along dimension 0
- grad_inducing: float32 [128, 8192], P(('group', 'lat'), 'sub'), parts along dimension 0
The draws below stay inside these ranges and needn't reach their ends.
There are 2 independent parts, one for each index of `group`. The reference program is written for one: setup_inputs(seed, part) draws one part's arguments, and reference() takes and returns one part's arrays. A program takes and returns all parts, laid end to end along the dimension named above; each array names one. Nothing has to cross between parts.
Inputs may be any that keep to these rules, and one draw needn't show every extreme that they name: Entry n indexes a row inside block n // 256 of the tables: cell n is table row (n // 256) * 512 + cell_index[n]; cells may repeat.
All inputs are finite; a program needn't handle non-finite values.
Results may differ from the reference program's by a relative error of at most 0.00075.
Values may be sent and summed in bfloat16 or wider, within the bound.
No kernel may reach another device: no remote copies, remote signals or barrier semaphores. Data moves between devices by JAX's collectives and lax.ppermute only.
A program may use at most 64 MiB of HBM per device.

```python
import math
import jax
import jax.numpy as jnp
from jax import lax

G = 16384
Q = 64
M = 8192
BAT_DEV = 256
TAB_DEV = 512
BATCH = 1024
TABLE = 2048


def plant(result, own_key, least, largest):
    place = [jax.random.randint(jax.random.fold_in(own_key, axis), (), 0, length) for axis, length in enumerate(result.shape)]
    main_axis = result.shape.index(max(result.shape))
    next_to = place[:main_axis] + [(place[main_axis] + 1) % result.shape[main_axis]] + place[main_axis + 1:]
    return result.at[tuple(place)].set(least).at[tuple(next_to)].set(largest)


def levels(own_key, extent, cuts, smallest, high):
    level = 1.0
    for position, shards_of in cuts:
        draws = jax.random.uniform(jax.random.fold_in(jax.random.fold_in(own_key, 6), position), (shards_of,), jnp.float32, smallest / len(cuts), high / len(cuts))
        level = level * jnp.repeat(jnp.exp(draws), extent[position] // shards_of).reshape((-1,) + (1,) * (len(extent) - 1 - position))
    return level


def gaussian(key, dims, width, reach, cuts=(), kind=jnp.bfloat16):
    result = jax.random.normal(key, dims, jnp.float32) * width
    if len(cuts) > 0:
        result = levels(key, dims, cuts, -0.22, 0.18) * result
    return jnp.clip(result, min=-reach, max=reach).astype(kind)


def setup_inputs(seed: int = 0, part: int = 0) -> dict:
    keys = jax.random.split(jax.random.key(seed), 10)
    own_keys = jax.random.split(jax.random.fold_in(keys[9], part), 10)
    cell_index = plant(jax.random.randint(own_keys[0], (BATCH,), 0, TAB_DEV), jax.random.fold_in(own_keys[0], 1), 0, TAB_DEV - 1).astype(jnp.int32)
    coords_table = jnp.clip(1.0 * jax.random.uniform(own_keys[1], (2, TABLE), jnp.float32) ** levels(own_keys[1], (2, TABLE), ((1, 4),), -0.2, 0.2), 0.0, 1.0)
    expr_table = gaussian(own_keys[2], (TABLE, G), 1.0, 6.0, ((0, 4), (1, 4)))
    inducing = jnp.clip(1.0 * jax.random.uniform(own_keys[3], (2, Q, M), jnp.float32) ** levels(own_keys[3], (2, Q, M), ((1, 2), (2, 2)), -0.2, 0.2), 0.0, 1.0)
    ind_weights = gaussian(own_keys[4], (Q, M), 0.1, 0.6, ((0, 2), (1, 2)), jnp.float32)
    lengthscale = jnp.clip(jnp.exp(math.log(0.1) - 1.609438 * jax.random.uniform(own_keys[5], (Q,), jnp.float32) ** levels(own_keys[5], (Q,), ((0, 2),), -0.2, 0.2)), 0.02, 0.1)
    variance = jnp.clip(jnp.exp(math.log(2.0) - 1.3862944 * jax.random.uniform(own_keys[6], (Q,), jnp.float32) ** levels(own_keys[6], (Q,), ((0, 2),), -0.2, 0.2)), 0.5, 2.0)
    mixing = gaussian(own_keys[7], (Q, G), Q ** -0.5, 0.75, ((1, 4),))
    noise_prec = jnp.clip(jnp.exp(math.log(4.0) - 2.0794415 * jax.random.uniform(own_keys[8], (G,), jnp.float32) ** levels(own_keys[8], (G,), ((0, 4),), -0.2, 0.2)), 0.5, 4.0)
    return dict(cell_index=cell_index, coords_table=coords_table, expr_table=expr_table, inducing=inducing, ind_weights=ind_weights, lengthscale=lengthscale, variance=variance, mixing=mixing, noise_prec=noise_prec)


def kernel_tile(cell_xy, points, length, height):
    delta_x = cell_xy[0][:, None] - points[0][None, :]
    delta_y = cell_xy[1][:, None] - points[1][None, :]
    return height * jnp.exp(-(delta_x * delta_x + delta_y * delta_y) * (0.5 / (length * length)))

def reference(cell_index, coords_table, expr_table, inducing, ind_weights, lengthscale, variance, mixing, noise_prec):
    cell_count = cell_index.shape[0]
    block_start = jnp.arange(cell_count, dtype=jnp.int32) // BAT_DEV * TAB_DEV
    table_rows = block_start + cell_index.astype(jnp.int32)
    cell_xy = jnp.take(coords_table, table_rows, axis=1)
    observed = jnp.take(expr_table, table_rows, axis=0)
    moved = jnp.moveaxis(inducing, 1, 0)

    def forward(packed):
        points, weights, length, height = packed
        return jnp.dot(kernel_tile(cell_xy, points, length, height), weights, precision=lax.Precision.HIGHEST)
    latent = lax.map(forward, (moved, ind_weights, lengthscale, variance)).astype(jnp.bfloat16)
    predicted = lax.dot_general(latent, mixing, (((0,), (0,)), ((), ())), preferred_element_type=jnp.float32)
    weighted = (noise_prec[None, :] * (observed.astype(jnp.float32) - predicted)).astype(jnp.bfloat16)
    grad_scale = -1.0 / math.sqrt(cell_count)
    grad_mixing = grad_scale * jnp.dot(latent, weighted, preferred_element_type=jnp.float32)
    latent_grad = grad_scale * lax.dot_general(mixing, weighted, (((1,), (1,)), ((), ())), preferred_element_type=jnp.float32)

    def backward(packed):
        points, gradient, length, height = packed
        return jnp.dot(gradient, kernel_tile(cell_xy, points, length, height), precision=lax.Precision.HIGHEST)
    grad_inducing = lax.map(backward, (moved, latent_grad, lengthscale, variance))
    return (grad_mixing, grad_inducing)
```

```python
import functools
import math

import jax
import jax.numpy as jnp
from jax import lax
from jax.experimental import pallas as pl
from jax.experimental.pallas import tpu as pltpu
from jax.sharding import PartitionSpec as P

LOG2E = math.log2(math.e)

def row_of(shape):
    return lax.broadcasted_iota(jnp.int32, shape, 0)

def parts(u, w, a):
    L = u.shape[1]
    U = (u - 0.5) * a
    W = (w - 0.5) * a
    big = 1.5 * 2.0**20
    U1 = (U + big) - big
    W1 = (W + big) - big
    rU = U - U1
    rW = W - W1
    hi = U1 * U1 + W1 * W1
    lo = rU * (U1 + U) + rW * (W1 + W)
    r = row_of((8, L)) % 4
    T = jnp.where(r == 0, U, jnp.where(r == 1, W, jnp.where(r == 2, hi, lo)))
    rc = row_of((8, 1)) % 4
    magic = jnp.where(rc <= 1, 1.5 * 2.0**20, jnp.where(rc == 2, 1.5 * 2.0**26, 1.5 * 2.0**18)).astype(jnp.float32)
    T1 = ((T + magic) - magic).astype(jnp.bfloat16).astype(jnp.float32)
    R = T - T1
    T2 = R.astype(jnp.bfloat16).astype(jnp.float32)
    T3 = R - T2
    return T1, T2, T3

def point_rows(u, w, a):
    T1, T2, T3 = parts(u, w, a)
    one = jnp.ones_like(T1)
    return jnp.concatenate([T1, T1, T2, T2, T1, T2, T3, T3, one, jnp.zeros_like(one)], 0).astype(jnp.bfloat16)

def cell_rows(u, w, a):
    T1, T2, T3 = parts(u, w, a)
    r8 = row_of(T1.shape)
    r = r8 % 4
    xy = r <= 1
    A1 = jnp.where(xy, 2 * T1, -1.0)
    A2 = jnp.where(xy, 2 * T2, 0.0)
    A3 = jnp.where(xy, 2 * T3, 0.0)
    outs = []
    for k in range(2):
        mine = (r8 // 4) == k
        G = [jnp.where(mine, A, 0.0) for A in (A1, A2, A3)]
        def n(T, i):
            return -T[4 * k + i : 4 * k + i + 1]
        z = jnp.zeros_like(n(T1, 0))
        norm = jnp.concatenate([n(T1, 2), n(T2, 2), n(T1, 3), n(T2, 3), n(T3, 3), z, z, z], 0)
        G1, G2, G3 = G
        outs.append(jnp.concatenate([G1, G2, G1, G2, G3, G3, G1, G2, norm, jnp.zeros_like(norm)], 0))
    return outs

def fwd_kernel(scale_ref, var_ref, pts_ref, w_ref, xy_ref, out_ref, rhs, lhs, acc, *, NB, MB, SB):
    p = pl.program_id(0)
    q = 2 * p
    M = pts_ref.shape[2]
    N = xy_ref.shape[1]
    r81 = row_of((8, 1))
    a = jnp.where(r81 < 4, scale_ref[q], scale_ref[q + 1])
    CH = 512
    def build(i, _):
        s = pl.ds(pl.multiple_of(i * CH, CH), CH)
        a0 = pts_ref[0, pl.ds(q, 1), s]; b0 = pts_ref[0, pl.ds(q + 1, 1), s]
        a1 = pts_ref[1, pl.ds(q, 1), s]; b1 = pts_ref[1, pl.ds(q + 1, 1), s]
        m = row_of((8, CH)) < 4
        rhs[:, s] = point_rows(jnp.where(m, a0, b0), jnp.where(m, a1, b1), a)
        return 0
    lax.fori_loop(0, M // CH, build, 0)
    cu = jnp.broadcast_to(xy_ref[0:1, :], (8, N))
    cw = jnp.broadcast_to(xy_ref[1:2, :], (8, N))
    L0, L1 = cell_rows(cu, cw, a)
    lhs[0] = L0.T.astype(jnp.bfloat16)
    lhs[1] = L1.T.astype(jnp.bfloat16)
    for k in range(2):
        acc[...] = jnp.zeros_like(acc)
        def step(i, _):
            base = i * MB
            for nb in range(N // NB):
                X = lhs[k, nb * NB:(nb + 1) * NB, :]
                t = acc[nb * NB:(nb + 1) * NB, :]
                for j in range(MB // SB):
                    s = pl.ds(pl.multiple_of(base + j * SB, SB), SB)
                    E = jnp.dot(X, rhs[:, s], preferred_element_type=jnp.float32)
                    e = jnp.exp2(E) * w_ref[pl.ds(q + k, 1), s]
                    for c in range(SB // 128):
                        t = t + e[:, c * 128:(c + 1) * 128]
                acc[nb * NB:(nb + 1) * NB, :] = t
            return 0
        lax.fori_loop(0, M // MB, step, 0)
        res = lax.dot_general(jnp.ones((8, 128), jnp.float32), acc[...], (((1,), (1,)), ((), ())),
                              precision=lax.Precision.HIGHEST, preferred_element_type=jnp.float32)
        out_ref[pl.ds(q + k, 1), :] = res[0:1] * var_ref[q + k]

def fwd(scale, var, pts, w, xy, NB=256, MB=1024, SB=512):
    _, Q, M = pts.shape
    N = xy.shape[1]
    return pl.pallas_call(
        functools.partial(fwd_kernel, NB=NB, MB=MB, SB=SB),
        grid=(Q // 2,),
        out_shape=jax.ShapeDtypeStruct((Q, N), jnp.float32),
        in_specs=[pl.BlockSpec(memory_space=pltpu.SMEM)] * 2 + [pl.BlockSpec(memory_space=pltpu.VMEM)] * 3,
        out_specs=pl.BlockSpec(memory_space=pltpu.VMEM),
        scratch_shapes=[pltpu.VMEM((80, M), jnp.bfloat16), pltpu.VMEM((2, N, 80), jnp.bfloat16), pltpu.VMEM((N, 128), jnp.float32)],
        compiler_params=pltpu.CompilerParams(vmem_limit_bytes=48 << 20),
        name="forward",
    )(scale, var, pts, w, xy)

def bwd_kernel(scale_ref, var_ref, pts_ref, lg_ref, xy_ref, out_ref, rhs, lhs, lgb, *, NB, MB, MI):
    p = pl.program_id(0)
    q = 2 * p
    M = pts_ref.shape[2]
    N = xy_ref.shape[1]
    r81 = row_of((8, 1))
    a = jnp.where(r81 < 4, scale_ref[q], scale_ref[q + 1])
    CH = 512
    def build(i, _):
        s = pl.ds(pl.multiple_of(i * CH, CH), CH)
        a0 = pts_ref[0, pl.ds(q, 1), s]; b0 = pts_ref[0, pl.ds(q + 1, 1), s]
        a1 = pts_ref[1, pl.ds(q, 1), s]; b1 = pts_ref[1, pl.ds(q + 1, 1), s]
        m = row_of((8, CH)) < 4
        rhs[:, s] = point_rows(jnp.where(m, a0, b0), jnp.where(m, a1, b1), a)
        return 0
    lax.fori_loop(0, M // CH, build, 0)
    cu = jnp.broadcast_to(xy_ref[0:1, :], (8, N))
    cw = jnp.broadcast_to(xy_ref[1:2, :], (8, N))
    L0, L1 = cell_rows(cu, cw, a)
    lhs[0] = L0.T.astype(jnp.bfloat16)
    lhs[1] = L1.T.astype(jnp.bfloat16)
    for k in range(2):
        lgb[...] = jnp.broadcast_to(lg_ref[pl.ds(q + k, 1), :], (128, N)).T
        def step(i, _):
            for j in range(MI):
                s = pl.ds(pl.multiple_of((i * MI + j) * MB, MB), MB)
                R = rhs[:, s]
                accs = [jnp.zeros((8, 128), jnp.float32) for _ in range(MB // 128)]
                for nb in range(N // NB):
                    X = lhs[k, nb * NB:(nb + 1) * NB, :]
                    E = jnp.dot(X, R, preferred_element_type=jnp.float32)
                    e = jnp.exp2(E)
                    g = lgb[nb * NB:(nb + 1) * NB, :]
                    for c in range(MB // 128):
                        pr = (e[:, c * 128:(c + 1) * 128] * g).reshape(NB // 8, 8, 128)
                        accs[c] = accs[c] + jnp.sum(pr, 0)
                row = jnp.concatenate([jnp.sum(x, 0, keepdims=True) for x in accs], 1)
                out_ref[pl.ds(q + k, 1), s] = row * var_ref[q + k]
            return 0
        lax.fori_loop(0, M // (MB * MI), step, 0)

def bwd(scale, var, pts, lg, xy, NB=256, MB=1024, MI=1):
    _, Q, M = pts.shape
    N = xy.shape[1]
    return pl.pallas_call(
        functools.partial(bwd_kernel, NB=NB, MB=MB, MI=MI),
        grid=(Q // 2,),
        out_shape=jax.ShapeDtypeStruct((Q, M), jnp.float32),
        in_specs=[pl.BlockSpec(memory_space=pltpu.SMEM)] * 2 + [pl.BlockSpec(memory_space=pltpu.VMEM)] * 3,
        out_specs=pl.BlockSpec(memory_space=pltpu.VMEM),
        scratch_shapes=[pltpu.VMEM((80, M), jnp.bfloat16), pltpu.VMEM((2, N, 80), jnp.bfloat16), pltpu.VMEM((N, 128), jnp.float32)],
        compiler_params=pltpu.CompilerParams(vmem_limit_bytes=48 << 20),
        name="backward",
    )(scale, var, pts, lg, xy)


def middle_kernel(idx_ref, latent_ref, mixing_ref, noise_ref, expr_ref, grad_ref, cell_ref, hot, *, scale):
    @pl.when(pl.program_id(0) == 0)
    def _():
        rows = lax.broadcasted_iota(jnp.int32, hot.shape, 1)
        hot[...] = jnp.where(rows == idx_ref[...], 1.0, 0.0).astype(jnp.bfloat16)
        cell_ref[...] = jnp.zeros_like(cell_ref)

    observed = jnp.dot(hot[...], expr_ref[...], preferred_element_type=jnp.float32)
    predicted = lax.dot_general(
        latent_ref[...], mixing_ref[...], (((0,), (0,)), ((), ())), preferred_element_type=jnp.float32
    )
    weighted = (noise_ref[...] * (observed - predicted)).astype(jnp.bfloat16)
    grad_ref[...] = scale * jnp.dot(latent_ref[...], weighted, preferred_element_type=jnp.float32)
    cell_ref[...] += scale * lax.dot_general(
        mixing_ref[...], weighted, (((1,), (1,)), ((), ())), preferred_element_type=jnp.float32
    )


def middle(idx, latent, mixing, noise, expr, scale):
    q, cells = latent.shape
    rows, genes = expr.shape
    width = math.gcd(genes, 512)
    return pl.pallas_call(
        functools.partial(middle_kernel, scale=scale),
        grid=(genes // width,),
        out_shape=(
            jax.ShapeDtypeStruct((q, genes), jnp.float32),
            jax.ShapeDtypeStruct((q, cells), jnp.float32),
        ),
        in_specs=[
            pl.BlockSpec((cells, 1), lambda i: (0, 0)),
            pl.BlockSpec((q, cells), lambda i: (0, 0)),
            pl.BlockSpec((q, width), lambda i: (0, i)),
            pl.BlockSpec((1, width), lambda i: (0, i)),
            pl.BlockSpec((rows, width), lambda i: (0, i)),
        ],
        out_specs=(
            pl.BlockSpec((q, width), lambda i: (0, i)),
            pl.BlockSpec((q, cells), lambda i: (0, 0)),
        ),
        scratch_shapes=[pltpu.VMEM((cells, rows), jnp.bfloat16)],
        compiler_params=pltpu.CompilerParams(vmem_limit_bytes=32 << 20),
        name="middle",
    )(idx, latent, mixing, noise, expr)


def on_device(cell_index, coords_table, expr_table, inducing, ind_weights, lengthscale, variance, mixing, noise_prec):
    genes, lats, subs = (lax.axis_size(name) for name in ("gene", "lat", "sub"))
    blocks = lats * subs
    cells = cell_index.shape[0]
    local_q = ind_weights.shape[0]
    points = ind_weights.shape[1]
    latent_cuts = math.gcd(genes, local_q // 2)
    cell_cuts = genes // latent_cuts
    own_q = local_q // latent_cuts
    part = cells // cell_cuts
    place = lax.axis_index("gene")
    first_q = place // cell_cuts * own_q
    every = ("gene", "lat", "sub")

    local_xy = jnp.take(coords_table, cell_index, axis=1)
    every_xy = lax.all_gather(local_xy, ("lat", "sub"), axis=1, tiled=True)
    every_xy = every_xy.reshape(2, blocks, cell_cuts, part)
    kernel_xy = lax.dynamic_slice_in_dim(every_xy, place % cell_cuts, 1, 2).reshape(2, blocks * part)
    own = functools.partial(lax.dynamic_slice_in_dim, start_index=first_q, slice_size=own_q)
    own_points = own(inducing, axis=1)
    own_weights = own(ind_weights, axis=0)
    own_scale = math.sqrt(0.5 * LOG2E) / own(lengthscale, axis=0)
    own_variance = own(variance, axis=0)

    partial = fwd(own_scale, own_variance, own_points, own_weights, kernel_xy)
    partial = partial.reshape(own_q, blocks, part).transpose(1, 0, 2)
    partial = jnp.broadcast_to(partial[None], (genes, blocks, own_q, part))
    partial = partial.reshape(genes * blocks, own_q, part)
    pieces = lax.all_to_all(partial, every, 0, 0, tiled=True)
    pieces = pieces.reshape(latent_cuts, cell_cuts, lats, subs, own_q, part).sum(3).astype(jnp.bfloat16)
    latent = pieces.transpose(2, 0, 3, 1, 4).reshape(lats * local_q, cells)

    grad_scale = -1.0 / math.sqrt(cells * blocks)
    mixing_term, cell_term = middle(
        cell_index[:, None], latent, mixing, noise_prec[None, :], expr_table, grad_scale
    )
    grad_mixing = lax.psum(mixing_term, ("lat", "sub"))

    send = cell_term.reshape(lats, latent_cuts, own_q, cell_cuts, part).transpose(1, 3, 0, 2, 4)
    send = jnp.broadcast_to(send[:, :, :, None], (latent_cuts, cell_cuts, lats, subs, own_q, part))
    send = send.reshape(genes * blocks, own_q, part)
    pieces = lax.all_to_all(send, every, 0, 0, tiled=True)
    latent_grad = pieces.reshape(genes, blocks, own_q, part).sum(0).transpose(1, 0, 2)
    latent_grad = latent_grad.reshape(own_q, blocks * part)

    inducing_term = bwd(own_scale, own_variance, own_points, latent_grad, kernel_xy)
    gathered = lax.all_gather(inducing_term, "gene", axis=0, tiled=True)
    grad_inducing = gathered.reshape(latent_cuts, cell_cuts, own_q, points).sum(1)
    return (grad_mixing, grad_inducing.reshape(local_q, points))


def solution(mesh):
    in_specs = (
        P(("group", "lat", "sub")),
        P("group", ("lat", "sub")),
        P(("group", "lat", "sub"), "gene"),
        P("group", "lat", "sub"),
        P(("group", "lat"), "sub"),
        P(("group", "lat")),
        P(("group", "lat")),
        P("group", "gene"),
        P(("group", "gene")),
    )
    out_specs = (P("group", "gene"), P(("group", "lat"), "sub"))
    return jax.shard_map(
        on_device, mesh=mesh, in_specs=in_specs, out_specs=out_specs, check_vma=False
    )
```

```python
import functools
import math

import jax
import jax.numpy as jnp
from jax import lax
from jax.experimental import pallas as pl
from jax.experimental.pallas import tpu as pltpu
from jax.sharding import PartitionSpec as P

LOG2E = math.log2(math.e)

def row_of(shape):
    return lax.broadcasted_iota(jnp.int32, shape, 0)

def parts(u, w, a):
    L = u.shape[1]
    U = (u - 0.5) * a
    W = (w - 0.5) * a
    big = 1.5 * 2.0**20
    U1 = (U + big) - big
    W1 = (W + big) - big
    rU = U - U1
    rW = W - W1
    hi = U1 * U1 + W1 * W1
    lo = rU * (U1 + U) + rW * (W1 + W)
    r = row_of((8, L)) % 4
    T = jnp.where(r == 0, U, jnp.where(r == 1, W, jnp.where(r == 2, hi, lo)))
    rc = row_of((8, 1)) % 4
    magic = jnp.where(rc <= 1, 1.5 * 2.0**20, jnp.where(rc == 2, 1.5 * 2.0**26, 1.5 * 2.0**18)).astype(jnp.float32)
    T1 = ((T + magic) - magic).astype(jnp.bfloat16).astype(jnp.float32)
    R = T - T1
    T2 = R.astype(jnp.bfloat16).astype(jnp.float32)
    T3 = R - T2
    return T1, T2, T3

def point_rows(u, w, a):
    T1, T2, T3 = parts(u, w, a)
    one = jnp.ones_like(T1)
    return jnp.concatenate([T1, T1, T2, T2, T1, T2, T3, T3, one, jnp.zeros_like(one)], 0).astype(jnp.bfloat16)

def cell_rows(u, w, a):
    T1, T2, T3 = parts(u, w, a)
    r8 = row_of(T1.shape)
    r = r8 % 4
    xy = r <= 1
    A1 = jnp.where(xy, 2 * T1, -1.0)
    A2 = jnp.where(xy, 2 * T2, 0.0)
    A3 = jnp.where(xy, 2 * T3, 0.0)
    outs = []
    for k in range(2):
        mine = (r8 // 4) == k
        G = [jnp.where(mine, A, 0.0) for A in (A1, A2, A3)]
        def n(T, i):
            return -T[4 * k + i : 4 * k + i + 1]
        z = jnp.zeros_like(n(T1, 0))
        norm = jnp.concatenate([n(T1, 2), n(T2, 2), n(T1, 3), n(T2, 3), n(T3, 3), z, z, z], 0)
        G1, G2, G3 = G
        outs.append(jnp.concatenate([G1, G2, G1, G2, G3, G3, G1, G2, norm, jnp.zeros_like(norm)], 0))
    return outs

VMEM = pltpu.VMEM
SMEM = pltpu.SMEM


def whole(space):
    return pl.BlockSpec(memory_space=space)


def partner(place, step, blocks):
    if blocks & (blocks - 1) == 0:
        return place ^ step
    return (place + step) % blocks


def locate_kernel(index_ref, table_ref, out_ref):
    table = table_ref[...]
    rows = table.shape[1]
    column = jnp.concatenate([table, jnp.zeros((8 - table.shape[0], rows), jnp.float32)], 0).T
    hot = lax.broadcasted_iota(jnp.int32, (rows, index_ref.shape[1]), 0) == index_ref[...]
    picked = [
        jnp.sum(jnp.where(hot, column[:, axis : axis + 1], 0.0), 0, keepdims=True)
        for axis in range(table.shape[0])
    ]
    out_ref[...] = jnp.concatenate(picked, 0)


def locate(index, table):
    return pl.pallas_call(
        locate_kernel,
        out_shape=jax.ShapeDtypeStruct((table.shape[0], index.shape[0]), jnp.float32),
        name="locate",
    )(index[None, :], table)


def scale_of(length_ref, q):
    lengths = jnp.where(row_of((8, 1)) < 4, length_ref[q], length_ref[q + 1])
    return math.sqrt(0.5 * LOG2E) / lengths


def build_kernel(first_ref, length_ref, points_ref, rhs_ref):
    q = first_ref[0] + 2 * pl.program_id(0)
    scale = scale_of(length_ref, q)
    width = math.gcd(points_ref.shape[2], 512)

    def step(i, _):
        s = pl.ds(pl.multiple_of(i * width, width), width)
        low = row_of((8, width)) < 4
        u, w = (
            jnp.where(low, points_ref[d, pl.ds(q, 1), s], points_ref[d, pl.ds(q + 1, 1), s]) for d in (0, 1)
        )
        rhs_ref[0, :, s] = point_rows(u, w, scale)
        return 0

    lax.fori_loop(0, points_ref.shape[2] // width, step, 0)


def build(first, lengths, points, own_q):
    count = points.shape[2]
    return pl.pallas_call(
        build_kernel,
        grid=(own_q // 2,),
        out_shape=jax.ShapeDtypeStruct((own_q // 2, 80, count), jnp.bfloat16),
        in_specs=[whole(SMEM), whole(SMEM), whole(VMEM)],
        out_specs=pl.BlockSpec((1, 80, count), lambda i: (i, 0, 0)),
        compiler_params=pltpu.CompilerParams(vmem_limit_bytes=16 << 20),
        cost_estimate=pl.CostEstimate(flops=4_000_000_000, bytes_accessed=4_000_000, transcendentals=0),
        name="build",
    )(first, lengths, points)


def forward_kernel(first_ref, order_ref, length_ref, var_ref, weight_ref, rhs_ref, *rest, blocks, NB, SB):
    xy_refs, (out_ref, lhs_ref, acc) = rest[:blocks], rest[blocks:]
    local = 2 * pl.program_id(0)
    q = first_ref[0] + local
    points = rhs_ref.shape[2]
    part = xy_refs[0].shape[1]
    cells = blocks * part
    scale = scale_of(length_ref, q)
    u, w = (
        jnp.broadcast_to(jnp.concatenate([ref[d : d + 1, :] for ref in xy_refs], 1), (8, cells)) for d in (0, 1)
    )
    for k, rows in enumerate(cell_rows(u, w, scale)):
        lhs_ref[0, k] = rows.T.astype(jnp.bfloat16)

    def latent(k, _):
        for nb in range(cells // NB):
            rows = slice(nb * NB, (nb + 1) * NB)
            cell = lhs_ref[0, k, rows, :]
            total = jnp.zeros((NB, 128), jnp.float32)
            for j in range(points // SB):
                s = slice(j * SB, (j + 1) * SB)
                e = jnp.exp2(jnp.dot(cell, rhs_ref[0, :, s], preferred_element_type=jnp.float32))
                weight = weight_ref[pl.ds(q + k, 1), s]
                for c in range(SB // 128):
                    total = total + e[:, c * 128 : (c + 1) * 128] * weight[:, c * 128 : (c + 1) * 128]
            acc[rows, :] = total
        result = lax.dot_general(
            jnp.ones((8, 128), jnp.float32),
            acc[...],
            (((1,), (1,)), ((), ())),
            precision=lax.Precision.HIGHEST,
            preferred_element_type=jnp.float32,
        )
        result = result[0:1] * var_ref[q + k]
        for b in range(blocks):
            for copy in range(out_ref.shape[0]):
                out_ref[copy, order_ref[b], pl.ds(local + k, 1), :] = result[:, b * part : (b + 1) * part]
        return 0

    lax.fori_loop(0, 2, latent, 0)


def forward(first, order, lengths, var, weights, rhs, xys, own_q, copies):
    points = rhs.shape[2]
    blocks = len(xys)
    part = xys[0].shape[1]
    cells = blocks * part
    return pl.pallas_call(
        functools.partial(forward_kernel, blocks=blocks, NB=math.gcd(cells, 256), SB=math.gcd(points, 512)),
        grid=(own_q // 2,),
        out_shape=(
            jax.ShapeDtypeStruct((copies, blocks, own_q, part), jnp.float32),
            jax.ShapeDtypeStruct((own_q // 2, 2, cells, 80), jnp.bfloat16),
        ),
        in_specs=[whole(SMEM)] * 4
        + [whole(VMEM), pl.BlockSpec((1, 80, points), lambda i: (i, 0, 0))]
        + [whole(VMEM)] * blocks,
        out_specs=(whole(VMEM), pl.BlockSpec((1, 2, cells, 80), lambda i: (i, 0, 0, 0))),
        scratch_shapes=[VMEM((cells, 128), jnp.float32)],
        compiler_params=pltpu.CompilerParams(vmem_limit_bytes=24 << 20),
        cost_estimate=pl.CostEstimate(flops=25_000_000_000, bytes_accessed=4_000_000, transcendentals=0),
        name="forward",
    )(first, order, lengths, var, weights, rhs, *xys)


def backward_kernel(first_ref, order_ref, var_ref, grad_ref, rhs_ref, lhs_ref, out_ref, held, spread, *, NB):
    local = 2 * pl.program_id(0)
    q = first_ref[0] + local
    points = rhs_ref.shape[2]
    copies, blocks, _, part = grad_ref.shape
    cells = blocks * part

    @pl.when(pl.program_id(0) == 0)
    def _():
        for b in range(blocks):
            held[b] = functools.reduce(jnp.add, [grad_ref[copy, order_ref[b]] for copy in range(copies)])

    def latent(k, _):
        for b in range(blocks):
            row = held[b, pl.ds(local + k, 1), :]
            spread[b * part : (b + 1) * part, :] = jnp.broadcast_to(row, (128, part)).T
        totals = [jnp.zeros((8, 128), jnp.float32) for _ in range(points // 128)]
        for nb in range(cells // NB):
            rows = slice(nb * NB, (nb + 1) * NB)
            cell = lhs_ref[0, k, rows, :]
            e = jnp.exp2(jnp.dot(cell, rhs_ref[0], preferred_element_type=jnp.float32))
            grad = spread[rows, :]
            for c in range(points // 128):
                term = (e[:, c * 128 : (c + 1) * 128] * grad).reshape(NB // 8, 8, 128)
                totals[c] = totals[c] + jnp.sum(term, 0)
        row = jnp.concatenate([jnp.sum(total, 0, keepdims=True) for total in totals], 1)
        out_ref[pl.ds(local + k, 1), :] = row * var_ref[q + k]
        return 0

    lax.fori_loop(0, 2, latent, 0)


def backward(first, order, var, grads, rhs, lhs):
    pairs, _, points = rhs.shape
    _, blocks, own_q, part = grads.shape
    cells = blocks * part
    return pl.pallas_call(
        functools.partial(backward_kernel, NB=math.gcd(cells, 256)),
        grid=(pairs,),
        out_shape=jax.ShapeDtypeStruct((own_q, points), jnp.float32),
        in_specs=[whole(SMEM)] * 3
        + [
            whole(VMEM),
            pl.BlockSpec((1, 80, points), lambda i: (i, 0, 0)),
            pl.BlockSpec((1, 2, cells, 80), lambda i: (i, 0, 0, 0)),
        ],
        out_specs=whole(VMEM),
        scratch_shapes=[VMEM((blocks, own_q, part), jnp.float32), VMEM((cells, 128), jnp.float32)],
        compiler_params=pltpu.CompilerParams(vmem_limit_bytes=24 << 20),
        cost_estimate=pl.CostEstimate(flops=25_000_000_000, bytes_accessed=4_000_000, transcendentals=0),
        name="backward",
    )(first, order, var, grads, rhs, lhs)


def observe_kernel(index_ref, expr_ref, out_ref, hot):
    @pl.when(pl.program_id(0) == 0)
    def _():
        rows = lax.broadcasted_iota(jnp.int32, hot.shape, 1)
        hot[...] = jnp.where(rows == index_ref[...], 1.0, 0.0).astype(jnp.bfloat16)

    picked = jnp.dot(hot[...], expr_ref[...], preferred_element_type=jnp.float32)
    out_ref[...] = picked.astype(jnp.bfloat16)


def observe(index, expr):
    rows, genes = expr.shape
    cells = index.shape[0]
    width = math.gcd(genes, 1024)
    return pl.pallas_call(
        observe_kernel,
        grid=(genes // width,),
        out_shape=jax.ShapeDtypeStruct((cells, genes), jnp.bfloat16),
        in_specs=[pl.BlockSpec((cells, 1), lambda i: (0, 0)), pl.BlockSpec((rows, width), lambda i: (0, i))],
        out_specs=pl.BlockSpec((cells, width), lambda i: (0, i)),
        scratch_shapes=[VMEM((cells, rows), jnp.bfloat16)],
        compiler_params=pltpu.CompilerParams(vmem_limit_bytes=16 << 20),
        cost_estimate=pl.CostEstimate(flops=3_000_000_000, bytes_accessed=6_000_000, transcendentals=0),
        name="observe",
    )(index[:, None], expr)


def middle_kernel(piece_ref, mixing_ref, noise_ref, observed_ref, grad_ref, send_ref, wide, *, scale, cuts, width):
    latent_cuts, cell_cuts, lats, subs = cuts
    own_q, part = piece_ref.shape[2:]
    for lat in range(lats):
        for a in range(latent_cuts):
            for b in range(cell_cuts):
                pieces = [piece_ref[a * cell_cuts + b, lat * subs + sub] for sub in range(subs)]
                first = (lat * latent_cuts + a) * own_q
                wide[first : first + own_q, b * part : (b + 1) * part] = functools.reduce(jnp.add, pieces)
    latent = wide[...].astype(jnp.bfloat16)
    turned = wide[...].T.astype(jnp.bfloat16)
    total = jnp.zeros(latent.shape, jnp.float32)
    for j in range(mixing_ref.shape[1] // width):
        s = slice(j * width, (j + 1) * width)
        predicted = jnp.dot(turned, mixing_ref[:, s], preferred_element_type=jnp.float32)
        observed = observed_ref[:, s].astype(jnp.float32)
        weighted = (noise_ref[:, s] * (observed - predicted)).astype(jnp.bfloat16)
        grad_ref[:, s] = scale * jnp.dot(latent, weighted, preferred_element_type=jnp.float32)
        total = total + lax.dot_general(
            mixing_ref[:, s], weighted, (((1,), (1,)), ((), ())), preferred_element_type=jnp.float32
        )
    wide[...] = scale * total
    for lat in range(lats):
        for a in range(latent_cuts):
            for b in range(cell_cuts):
                first = (lat * latent_cuts + a) * own_q
                piece = wide[first : first + own_q, b * part : (b + 1) * part]
                for sub in range(subs):
                    send_ref[a * cell_cuts + b, lat * subs + sub] = piece


def middle(pieces, mixing, noise, observed, scale, cuts):
    cells, genes = observed.shape
    q = mixing.shape[0]
    return pl.pallas_call(
        functools.partial(middle_kernel, scale=scale, cuts=cuts, width=math.gcd(genes, 512)),
        out_shape=(
            jax.ShapeDtypeStruct((q, genes), jnp.float32),
            jax.ShapeDtypeStruct(pieces.shape, jnp.float32),
        ),
        scratch_shapes=[VMEM((q, cells), jnp.float32)],
        compiler_params=pltpu.CompilerParams(vmem_limit_bytes=24 << 20),
        cost_estimate=pl.CostEstimate(flops=3_000_000_000, bytes_accessed=4_000_000, transcendentals=0),
        name="middle",
    )(pieces, mixing, noise[None, :], observed)


def shifted(x, axes, step, size):
    return lax.ppermute(x, axes, [(partner(i, step, size), i) for i in range(size)])


def sum_over(x, first_axis, then_axis):
    n = lax.axis_size(first_axis)
    m = lax.axis_size(then_axis)
    me = lax.axis_index(first_axis)
    rows = x.shape[0] // n

    def rows_of(place):
        return lax.dynamic_slice_in_dim(x, place * rows, rows, 0)

    total = rows_of(me)
    for step in range(1, n):
        to = me ^ step if n & (n - 1) == 0 else (me - step) % n
        total = total + shifted(rows_of(to), first_axis, step, n)
    total = functools.reduce(jnp.add, [total] + [shifted(total, then_axis, step, m) for step in range(1, m)])
    out = lax.dynamic_update_slice_in_dim(jnp.zeros_like(x), total, me * rows, 0)
    for step in range(1, n):
        out = lax.dynamic_update_slice_in_dim(
            out, shifted(total, first_axis, step, n), partner(me, step, n) * rows, 0
        )
    return out


def on_device(cell_index, coords_table, expr_table, inducing, ind_weights, lengthscale, variance, mixing, noise_prec):
    genes, lats, subs = (lax.axis_size(name) for name in ("gene", "lat", "sub"))
    blocks = lats * subs
    cells = cell_index.shape[0]
    local_q, points = ind_weights.shape
    latent_cuts = math.gcd(genes, local_q // 2)
    cell_cuts = genes // latent_cuts
    cuts = (latent_cuts, cell_cuts, lats, subs)
    own_q = local_q // latent_cuts
    part = cells // cell_cuts
    place = lax.axis_index("gene")
    block = lax.axis_index("lat") * subs + lax.axis_index("sub")
    first = (place // cell_cuts * own_q).reshape(1)
    order = jnp.stack([partner(block, step, blocks) for step in range(blocks)])
    every = ("gene", "lat", "sub")

    local_xy = locate(cell_index, coords_table)
    xys = [local_xy] + [shifted(local_xy, ("lat", "sub"), step, blocks) for step in range(1, blocks)]
    xys = [lax.dynamic_slice_in_dim(xy, place % cell_cuts * part, part, 1) for xy in xys]
    rhs = build(first, lengthscale, inducing, own_q)

    partial, lhs = forward(first, order, lengthscale, variance, ind_weights, rhs, xys, own_q, genes)
    expr_table, partial = lax.optimization_barrier((expr_table, partial))
    pieces = lax.all_to_all(partial.reshape(genes * blocks, own_q, part), every, 0, 0, tiled=True)
    observed = observe(cell_index, expr_table)

    grad_scale = -1.0 / math.sqrt(cells * blocks)
    mixing_term, send = middle(
        pieces.reshape(genes, blocks, own_q, part), mixing, noise_prec, observed, grad_scale, cuts
    )
    pieces = lax.all_to_all(send.reshape(genes * blocks, own_q, part), every, 0, 0, tiled=True)
    grad_mixing = sum_over(mixing_term, "sub", "lat")

    inducing_term = backward(first, order, variance, pieces.reshape(genes, blocks, own_q, part), rhs, lhs)
    gathered = lax.all_gather(inducing_term, "gene", axis=0, tiled=True)
    grad_inducing = gathered.reshape(latent_cuts, cell_cuts, own_q, points).sum(1)
    return (grad_mixing, grad_inducing.reshape(local_q, points))


def solution(mesh):
    in_specs = (
        P(("group", "lat", "sub")),
        P("group", ("lat", "sub")),
        P(("group", "lat", "sub"), "gene"),
        P("group", "lat", "sub"),
        P(("group", "lat"), "sub"),
        P(("group", "lat")),
        P(("group", "lat")),
        P("group", "gene"),
        P(("group", "gene")),
    )
    out_specs = (P("group", "gene"), P(("group", "lat"), "sub"))
    return jax.shard_map(
        on_device, mesh=mesh, in_specs=in_specs, out_specs=out_specs, check_vma=False
    )
```

```python
import functools
import math

import jax
import jax.numpy as jnp
from jax import lax
from jax.experimental import pallas as pl
from jax.experimental.pallas import tpu as pltpu
from jax.sharding import PartitionSpec as P

LOG2E = math.log2(math.e)
ROOM = 24 << 20

def row_of(shape):
    return lax.broadcasted_iota(jnp.int32, shape, 0)

def parts(u, w, a):
    L = u.shape[1]
    U = (u - 0.5) * a
    W = (w - 0.5) * a
    big = 1.5 * 2.0**20
    U1 = (U + big) - big
    W1 = (W + big) - big
    rU = U - U1
    rW = W - W1
    hi = U1 * U1 + W1 * W1
    lo = rU * (U1 + U) + rW * (W1 + W)
    r = row_of((8, L)) % 4
    T = jnp.where(r == 0, U, jnp.where(r == 1, W, jnp.where(r == 2, hi, lo)))
    rc = row_of((8, 1)) % 4
    magic = jnp.where(rc <= 1, 1.5 * 2.0**20, jnp.where(rc == 2, 1.5 * 2.0**26, 1.5 * 2.0**18)).astype(jnp.float32)
    T1 = ((T + magic) - magic).astype(jnp.bfloat16).astype(jnp.float32)
    R = T - T1
    T2 = R.astype(jnp.bfloat16).astype(jnp.float32)
    T3 = R - T2
    return T1, T2, T3

def point_rows(u, w, a):
    T1, T2, T3 = parts(u, w, a)
    one = jnp.ones_like(T1)
    return jnp.concatenate([T1, T1, T2, T2, T1, T2, T3, T3, one, jnp.zeros_like(one)], 0).astype(jnp.bfloat16)

def cell_rows(u, w, a):
    T1, T2, T3 = parts(u, w, a)
    r8 = row_of(T1.shape)
    r = r8 % 4
    xy = r <= 1
    A1 = jnp.where(xy, 2 * T1, -1.0)
    A2 = jnp.where(xy, 2 * T2, 0.0)
    A3 = jnp.where(xy, 2 * T3, 0.0)
    outs = []
    for k in range(2):
        mine = (r8 // 4) == k
        G = [jnp.where(mine, A, 0.0) for A in (A1, A2, A3)]
        def n(T, i):
            return -T[4 * k + i : 4 * k + i + 1]
        z = jnp.zeros_like(n(T1, 0))
        norm = jnp.concatenate([n(T1, 2), n(T2, 2), n(T1, 3), n(T2, 3), n(T3, 3), z, z, z], 0)
        G1, G2, G3 = G
        outs.append(jnp.concatenate([G1, G2, G1, G2, G3, G3, G1, G2, norm, jnp.zeros_like(norm)], 0))
    return outs

VMEM = pltpu.VMEM
SMEM = pltpu.SMEM


def whole(space):
    return pl.BlockSpec(memory_space=space)


def partner(place, step, blocks):
    if blocks & (blocks - 1) == 0:
        return place ^ step
    return (place + step) % blocks


def locate_kernel(index_ref, table_ref, out_ref):
    table = table_ref[...]
    rows = table.shape[1]
    column = jnp.concatenate([table, jnp.zeros((8 - table.shape[0], rows), jnp.float32)], 0).T
    hot = lax.broadcasted_iota(jnp.int32, (rows, index_ref.shape[1]), 0) == index_ref[...]
    picked = [
        jnp.sum(jnp.where(hot, column[:, axis : axis + 1], 0.0), 0, keepdims=True)
        for axis in range(table.shape[0])
    ]
    out_ref[...] = jnp.concatenate(picked, 0)


def locate(index, table):
    return pl.pallas_call(
        locate_kernel,
        out_shape=jax.ShapeDtypeStruct((table.shape[0], index.shape[0]), jnp.float32),
        name="locate",
    )(index[None, :], table)


def scale_of(length_ref, q):
    lengths = jnp.where(row_of((8, 1)) < 4, length_ref[q], length_ref[q + 1])
    return math.sqrt(0.5 * LOG2E) / lengths


def build_kernel(first_ref, length_ref, points_ref, rhs_ref):
    q = first_ref[0] + 2 * pl.program_id(0)
    scale = scale_of(length_ref, q)
    width = math.gcd(points_ref.shape[2], 512)

    def step(i, _):
        s = pl.ds(pl.multiple_of(i * width, width), width)
        low = row_of((8, width)) < 4
        u, w = (
            jnp.where(low, points_ref[d, pl.ds(q, 1), s], points_ref[d, pl.ds(q + 1, 1), s]) for d in (0, 1)
        )
        rhs_ref[0, :, s] = point_rows(u, w, scale)
        return 0

    lax.fori_loop(0, points_ref.shape[2] // width, step, 0)


def build(first, lengths, points, own_q):
    count = points.shape[2]
    return pl.pallas_call(
        build_kernel,
        grid=(own_q // 2,),
        out_shape=pltpu.HBM((own_q // 2, 80, count), jnp.bfloat16),
        in_specs=[whole(SMEM), whole(SMEM), whole(VMEM)],
        out_specs=pl.BlockSpec((1, 80, count), lambda i: (i, 0, 0)),
        compiler_params=pltpu.CompilerParams(vmem_limit_bytes=ROOM),
        cost_estimate=pl.CostEstimate(flops=4_000_000_000, bytes_accessed=4_000_000, transcendentals=0),
        name="build",
    )(first, lengths, points)


def forward_kernel(first_ref, order_ref, length_ref, var_ref, weight_ref, rhs_ref, *rest, blocks, NB, SB):
    xy_refs, (out_ref, lhs_ref, acc) = rest[:blocks], rest[blocks:]
    local = 2 * pl.program_id(0)
    q = first_ref[0] + local
    points = rhs_ref.shape[2]
    part = xy_refs[0].shape[1]
    cells = blocks * part
    scale = scale_of(length_ref, q)
    u, w = (
        jnp.broadcast_to(jnp.concatenate([ref[d : d + 1, :] for ref in xy_refs], 1), (8, cells)) for d in (0, 1)
    )
    for k, rows in enumerate(cell_rows(u, w, scale)):
        lhs_ref[0, k] = rows.T.astype(jnp.bfloat16)

    def latent(k, _):
        for nb in range(cells // NB):
            rows = slice(nb * NB, (nb + 1) * NB)
            cell = lhs_ref[0, k, rows, :]
            total = jnp.zeros((NB, 128), jnp.float32)
            for j in range(points // SB):
                s = slice(j * SB, (j + 1) * SB)
                e = jnp.exp2(jnp.dot(cell, rhs_ref[0, :, s], preferred_element_type=jnp.float32))
                weight = weight_ref[pl.ds(q + k, 1), s]
                for c in range(SB // 128):
                    total = total + e[:, c * 128 : (c + 1) * 128] * weight[:, c * 128 : (c + 1) * 128]
            acc[rows, :] = total
        high = acc[...].astype(jnp.bfloat16)
        rest = acc[...] - high.astype(jnp.float32)
        middle = rest.astype(jnp.bfloat16)
        low = (rest - middle.astype(jnp.float32)).astype(jnp.bfloat16)
        result = functools.reduce(
            jnp.add,
            [
                lax.dot_general(
                    jnp.ones((8, 128), jnp.bfloat16),
                    term,
                    (((1,), (1,)), ((), ())),
                    preferred_element_type=jnp.float32,
                )
                for term in (high, middle, low)
            ],
        )
        result = result[0:1] * var_ref[q + k]
        for b in range(blocks):
            for copy in range(out_ref.shape[0]):
                out_ref[copy, order_ref[b], pl.ds(local + k, 1), :] = result[:, b * part : (b + 1) * part]
        return 0

    lax.fori_loop(0, 2, latent, 0)


def forward(first, order, lengths, var, weights, rhs, xys, own_q, copies):
    points = rhs.shape[2]
    blocks = len(xys)
    part = xys[0].shape[1]
    cells = blocks * part
    return pl.pallas_call(
        functools.partial(forward_kernel, blocks=blocks, NB=math.gcd(cells, 256), SB=points),
        grid=(own_q // 2,),
        out_shape=(
            jax.ShapeDtypeStruct((copies, blocks, own_q, part), jnp.float32),
            pltpu.HBM((own_q // 2, 2, cells, 80), jnp.bfloat16),
        ),
        in_specs=[whole(SMEM)] * 4
        + [whole(VMEM), pl.BlockSpec((1, 80, points), lambda i: (i, 0, 0))]
        + [whole(VMEM)] * blocks,
        out_specs=(whole(VMEM), pl.BlockSpec((1, 2, cells, 80), lambda i: (i, 0, 0, 0))),
        scratch_shapes=[VMEM((cells, 128), jnp.float32)],
        compiler_params=pltpu.CompilerParams(vmem_limit_bytes=ROOM),
        cost_estimate=pl.CostEstimate(flops=25_000_000_000, bytes_accessed=4_000_000, transcendentals=0),
        name="forward",
    )(first, order, lengths, var, weights, pltpu.with_memory_space_constraint(rhs, pltpu.HBM), *xys)


def backward_kernel(first_ref, order_ref, var_ref, grad_ref, rhs_ref, lhs_ref, out_ref, held, spread, *, NB):
    local = 2 * pl.program_id(0)
    q = first_ref[0] + local
    points = rhs_ref.shape[2]
    copies, blocks, _, part = grad_ref.shape
    cells = blocks * part

    @pl.when(pl.program_id(0) == 0)
    def _():
        for b in range(blocks):
            held[b] = functools.reduce(jnp.add, [grad_ref[copy, order_ref[b]] for copy in range(copies)])

    def latent(k, _):
        for b in range(blocks):
            row = held[b, pl.ds(local + k, 1), :]
            spread[b * part : (b + 1) * part, :] = jnp.broadcast_to(row, (128, part)).T
        totals = [jnp.zeros((8, 128), jnp.float32) for _ in range(points // 128)]
        for nb in range(cells // NB):
            rows = slice(nb * NB, (nb + 1) * NB)
            cell = lhs_ref[0, k, rows, :]
            e = jnp.exp2(jnp.dot(cell, rhs_ref[0], preferred_element_type=jnp.float32))
            grad = spread[rows, :]
            for c in range(points // 128):
                term = (e[:, c * 128 : (c + 1) * 128] * grad).reshape(NB // 8, 8, 128)
                totals[c] = totals[c] + jnp.sum(term, 0)
        row = jnp.concatenate([jnp.sum(total, 0, keepdims=True) for total in totals], 1)
        out_ref[pl.ds(local + k, 1), :] = row * var_ref[q + k]
        return 0

    lax.fori_loop(0, 2, latent, 0)


def backward(first, order, var, grads, rhs, lhs):
    pairs, _, points = rhs.shape
    _, blocks, own_q, part = grads.shape
    cells = blocks * part
    return pl.pallas_call(
        functools.partial(backward_kernel, NB=math.gcd(cells, 256)),
        grid=(pairs,),
        out_shape=jax.ShapeDtypeStruct((own_q, points), jnp.float32),
        in_specs=[whole(SMEM)] * 3
        + [
            whole(VMEM),
            pl.BlockSpec((1, 80, points), lambda i: (i, 0, 0)),
            pl.BlockSpec((1, 2, cells, 80), lambda i: (i, 0, 0, 0)),
        ],
        out_specs=whole(VMEM),
        scratch_shapes=[VMEM((blocks, own_q, part), jnp.float32), VMEM((cells, 128), jnp.float32)],
        compiler_params=pltpu.CompilerParams(vmem_limit_bytes=ROOM),
        cost_estimate=pl.CostEstimate(flops=25_000_000_000, bytes_accessed=4_000_000, transcendentals=0),
        name="backward",
    )(first, order, var, grads, *(pltpu.with_memory_space_constraint(x, pltpu.HBM) for x in (rhs, lhs)))


def observe_kernel(index_ref, expr_hbm, out_hbm, expr_ref, out_ref, load_sem, store_sem):
    rows, genes = expr_ref.shape
    count, cells, width = out_ref.shape
    columns = [slice(j * width, (j + 1) * width) for j in range(genes // width)]
    loads = [
        pltpu.make_async_copy(expr_hbm.at[:, s], expr_ref.at[:, s], load_sem.at[j]) for j, s in enumerate(columns)
    ]
    for copy in loads:
        copy.start()
    places = lax.broadcasted_iota(jnp.int32, (cells, rows), 1)
    hot = jnp.where(places == index_ref[...], 1.0, 0.0).astype(jnp.bfloat16)
    stores = []
    for j, s in enumerate(columns):
        loads[j].wait()
        out_ref[j] = jnp.dot(hot, expr_ref[:, s], preferred_element_type=jnp.float32).astype(jnp.bfloat16)
        copy = pltpu.make_async_copy(out_ref.at[j], out_hbm.at[j], store_sem.at[j])
        copy.start()
        stores.append(copy)
    for copy in stores:
        copy.wait()


def observe(index, expr):
    rows, genes = expr.shape
    cells = index.shape[0]
    width = math.gcd(genes, 512)
    count = genes // width
    return pl.pallas_call(
        observe_kernel,
        out_shape=pltpu.HBM((count, cells, width), jnp.bfloat16),
        in_specs=[whole(VMEM), whole(pltpu.HBM)],
        out_specs=whole(pltpu.HBM),
        scratch_shapes=[
            VMEM((rows, genes), jnp.bfloat16),
            VMEM((count, cells, width), jnp.bfloat16),
            pltpu.SemaphoreType.DMA((count,)),
            pltpu.SemaphoreType.DMA((count,)),
        ],
        compiler_params=pltpu.CompilerParams(vmem_limit_bytes=ROOM),
        cost_estimate=pl.CostEstimate(flops=3_000_000_000, bytes_accessed=6_000_000, transcendentals=0),
        name="observe",
    )(index[:, None], pltpu.with_memory_space_constraint(expr, pltpu.HBM))


def middle_kernel(rows_ref, piece_ref, mixing_ref, noise_ref, observed_ref, *rest, scale, cuts, shares):
    grad_refs, (send_ref, wide, latent) = rest[:shares], rest[shares:]
    latent_cuts, cell_cuts, lats, subs = cuts
    own_q, part = piece_ref.shape[2:]
    count, _, width = observed_ref.shape
    share = mixing_ref.shape[0] // shares
    for lat in range(lats):
        for a in range(latent_cuts):
            for b in range(cell_cuts):
                pieces = [piece_ref[a * cell_cuts + b, lat * subs + sub] for sub in range(subs)]
                first = (lat * latent_cuts + a) * own_q
                wide[first : first + own_q, b * part : (b + 1) * part] = functools.reduce(jnp.add, pieces)
    latent[...] = wide[...].astype(jnp.bfloat16)
    turned = wide[...].T.astype(jnp.bfloat16)
    halves = [latent[pl.ds(pl.multiple_of(rows_ref[i] * share, share), share), :] for i in range(shares)]
    ordered = jnp.concatenate(halves, 0)
    total = jnp.zeros(latent.shape, jnp.float32)
    for j in range(count):
        s = slice(j * width, (j + 1) * width)
        predicted = jnp.dot(turned, mixing_ref[:, s], preferred_element_type=jnp.float32)
        observed = observed_ref[j].astype(jnp.float32)
        weighted = (noise_ref[:, s] * (observed - predicted)).astype(jnp.bfloat16)
        grads = scale * jnp.dot(ordered, weighted, preferred_element_type=jnp.float32)
        for i in range(shares):
            grad_refs[i][:, s] = grads[i * share : (i + 1) * share]
        total = total + lax.dot_general(
            mixing_ref[:, s], weighted, (((1,), (1,)), ((), ())), preferred_element_type=jnp.float32
        )
    wide[...] = scale * total
    for lat in range(lats):
        for a in range(latent_cuts):
            for b in range(cell_cuts):
                first = (lat * latent_cuts + a) * own_q
                piece = wide[first : first + own_q, b * part : (b + 1) * part]
                for sub in range(subs):
                    send_ref[a * cell_cuts + b, lat * subs + sub] = piece


def middle(rows, pieces, mixing, noise, observed, scale, cuts):
    count, cells, width = observed.shape
    q, genes = mixing.shape
    shares = rows.shape[0]
    return pl.pallas_call(
        functools.partial(middle_kernel, scale=scale, cuts=cuts, shares=shares),
        out_shape=(jax.ShapeDtypeStruct((q // shares, genes), jnp.float32),) * shares
        + (jax.ShapeDtypeStruct(pieces.shape, jnp.float32),),
        in_specs=[whole(SMEM)] + [whole(VMEM)] * 4,
        out_specs=(whole(VMEM),) * (shares + 1),
        scratch_shapes=[
            VMEM((q, cells), jnp.float32),
            VMEM((q, cells), jnp.bfloat16),
        ],
        compiler_params=pltpu.CompilerParams(vmem_limit_bytes=ROOM),
        cost_estimate=pl.CostEstimate(flops=3_000_000_000, bytes_accessed=4_000_000, transcendentals=0),
        name="middle",
    )(
        rows,
        pieces,
        mixing,
        noise[None, :],
        observed,
    )


def shifted(x, axes, step, size):
    return lax.ppermute(x, axes, [(partner(i, step, size), i) for i in range(size)])


def gather_rows(x, axis):
    n = lax.axis_size(axis)
    me = lax.axis_index(axis)
    rows = x.shape[0]
    out = lax.dynamic_update_slice_in_dim(jnp.zeros((n * rows, x.shape[1]), x.dtype), x, me * rows, 0)
    for step in range(1, n):
        out = lax.dynamic_update_slice_in_dim(out, shifted(x, axis, step, n), partner(me, step, n) * rows, 0)
    return out


def on_device(cell_index, coords_table, expr_table, inducing, ind_weights, lengthscale, variance, mixing, noise_prec):
    genes, lats, subs = (lax.axis_size(name) for name in ("gene", "lat", "sub"))
    blocks = lats * subs
    cells = cell_index.shape[0]
    local_q, points = ind_weights.shape
    latent_cuts = math.gcd(genes, local_q // 2)
    cell_cuts = genes // latent_cuts
    cuts = (latent_cuts, cell_cuts, lats, subs)
    own_q = local_q // latent_cuts
    part = cells // cell_cuts
    place = lax.axis_index("gene")
    block = lax.axis_index("lat") * subs + lax.axis_index("sub")
    first = (place // cell_cuts * own_q).reshape(1)
    order = jnp.stack([partner(block, step, blocks) for step in range(blocks)])
    every = ("gene", "lat", "sub")

    local_xy = locate(cell_index, coords_table)
    xys = [local_xy] + [shifted(local_xy, ("lat", "sub"), step, blocks) for step in range(1, blocks)]
    xys = [lax.dynamic_slice_in_dim(xy, place % cell_cuts * part, part, 1) for xy in xys]
    rhs = build(first, lengthscale, inducing, own_q)

    partial, lhs = forward(first, order, lengthscale, variance, ind_weights, rhs, xys, own_q, genes)
    late_index, partial = lax.optimization_barrier((cell_index, partial))
    pieces = lax.all_to_all(partial.reshape(genes * blocks, own_q, part), every, 0, 0, tiled=True)
    observed = observe(late_index, expr_table)

    grad_scale = -1.0 / math.sqrt(cells * blocks)
    sub = lax.axis_index("sub")
    rows = [sub ^ step if subs & (subs - 1) == 0 else (sub - step) % subs for step in range(subs)]
    *terms, send = middle(
        jnp.stack(rows), pieces.reshape(genes, blocks, own_q, part), mixing, noise_prec, observed, grad_scale, cuts
    )
    pieces = lax.all_to_all(send.reshape(genes * blocks, own_q, part), every, 0, 0, tiled=True)
    half = functools.reduce(
        jnp.add, [terms[0]] + [shifted(terms[step], "sub", step, subs) for step in range(1, subs)]
    )
    others = [shifted(half, "lat", step, lats) for step in range(1, lats)]

    inducing_term = backward(first, order, variance, pieces.reshape(genes, blocks, own_q, part), rhs, lhs)
    inducing_term, *others = lax.optimization_barrier((inducing_term, *others))
    grad_mixing = gather_rows(functools.reduce(jnp.add, others, half), "sub")
    gathered = lax.all_gather(inducing_term, "gene", axis=0, tiled=True)
    grad_inducing = gathered.reshape(latent_cuts, cell_cuts, own_q, points).sum(1)
    return (grad_mixing, grad_inducing.reshape(local_q, points))


def solution(mesh):
    in_specs = (
        P(("group", "lat", "sub")),
        P("group", ("lat", "sub")),
        P(("group", "lat", "sub"), "gene"),
        P("group", "lat", "sub"),
        P(("group", "lat"), "sub"),
        P(("group", "lat")),
        P(("group", "lat")),
        P("group", "gene"),
        P(("group", "gene")),
    )
    out_specs = (P("group", "gene"), P(("group", "lat"), "sub"))
    return jax.shard_map(
        on_device, mesh=mesh, in_specs=in_specs, out_specs=out_specs, check_vma=False
    )
```

```python
import functools
import math

import jax
import jax.numpy as jnp
from jax import lax
from jax.experimental import pallas as pl
from jax.experimental.pallas import tpu as pltpu
from jax.sharding import PartitionSpec as P

LOG2E = math.log2(math.e)
ROOM = 24 << 20

def row_of(shape):
    return lax.broadcasted_iota(jnp.int32, shape, 0)

def parts(u, w, a):
    L = u.shape[1]
    U = (u - 0.5) * a
    W = (w - 0.5) * a
    big = 1.5 * 2.0**20
    U1 = (U + big) - big
    W1 = (W + big) - big
    rU = U - U1
    rW = W - W1
    hi = U1 * U1 + W1 * W1
    lo = rU * (U1 + U) + rW * (W1 + W)
    r = row_of((8, L)) % 4
    T = jnp.where(r == 0, U, jnp.where(r == 1, W, jnp.where(r == 2, hi, lo)))
    rc = row_of((8, 1)) % 4
    magic = jnp.where(rc <= 1, 1.5 * 2.0**20, jnp.where(rc == 2, 1.5 * 2.0**26, 1.5 * 2.0**18)).astype(jnp.float32)
    T1 = ((T + magic) - magic).astype(jnp.bfloat16).astype(jnp.float32)
    R = T - T1
    T2 = R.astype(jnp.bfloat16).astype(jnp.float32)
    T3 = R - T2
    return T1, T2, T3

def point_rows(u, w, a):
    T1, T2, T3 = parts(u, w, a)
    one = jnp.ones_like(T1)
    return jnp.concatenate([T1, T1, T2, T2, T1, T2, T3, T3, one, jnp.zeros_like(one)], 0).astype(jnp.bfloat16)

def cell_rows(u, w, a):
    T1, T2, T3 = parts(u, w, a)
    r8 = row_of(T1.shape)
    r = r8 % 4
    xy = r <= 1
    A1 = jnp.where(xy, 2 * T1, -1.0)
    A2 = jnp.where(xy, 2 * T2, 0.0)
    A3 = jnp.where(xy, 2 * T3, 0.0)
    outs = []
    for k in range(2):
        mine = (r8 // 4) == k
        G = [jnp.where(mine, A, 0.0) for A in (A1, A2, A3)]
        def n(T, i):
            return -T[4 * k + i : 4 * k + i + 1]
        z = jnp.zeros_like(n(T1, 0))
        norm = jnp.concatenate([n(T1, 2), n(T2, 2), n(T1, 3), n(T2, 3), n(T3, 3), z, z, z], 0)
        G1, G2, G3 = G
        outs.append(jnp.concatenate([G1, G2, G1, G2, G3, G3, G1, G2, norm, jnp.zeros_like(norm)], 0))
    return outs

VMEM = pltpu.VMEM
SMEM = pltpu.SMEM


def whole(space):
    return pl.BlockSpec(memory_space=space)


def partner(place, step, blocks):
    if blocks & (blocks - 1) == 0:
        return place ^ step
    return (place + step) % blocks


def locate_kernel(index_ref, table_ref, out_ref):
    table = table_ref[...]
    rows = table.shape[1]
    column = jnp.concatenate([table, jnp.zeros((8 - table.shape[0], rows), jnp.float32)], 0).T
    hot = lax.broadcasted_iota(jnp.int32, (rows, index_ref.shape[1]), 0) == index_ref[...]
    picked = [
        jnp.sum(jnp.where(hot, column[:, axis : axis + 1], 0.0), 0, keepdims=True)
        for axis in range(table.shape[0])
    ]
    out_ref[...] = jnp.concatenate(picked, 0)


def locate(index, table):
    return pl.pallas_call(
        locate_kernel,
        out_shape=jax.ShapeDtypeStruct((table.shape[0], index.shape[0]), jnp.float32),
        name="locate",
    )(index[None, :], table)


def scale_of(length_ref, q):
    lengths = jnp.where(row_of((8, 1)) < 4, length_ref[q], length_ref[q + 1])
    return math.sqrt(0.5 * LOG2E) / lengths


def build_kernel(first_ref, length_ref, points_ref, rhs_ref, *, aligned):
    local = 2 * pl.program_id(0)
    scale = scale_of(length_ref, first_ref[0] + local)
    row = local if aligned else first_ref[0] + local
    width = math.gcd(points_ref.shape[2], 2048)

    def step(i, _):
        s = pl.ds(pl.multiple_of(i * width, width), width)
        low = row_of((8, width)) < 4
        u, w = (
            jnp.where(low, points_ref[d, pl.ds(row, 1), s], points_ref[d, pl.ds(row + 1, 1), s]) for d in (0, 1)
        )
        rhs_ref[0, :, s] = point_rows(u, w, scale)
        return 0

    lax.fori_loop(0, points_ref.shape[2] // width, step, 0)


def build(first, lengths, points, own_q):
    axes, local_q, count = points.shape
    aligned = own_q % 8 == 0
    block = (axes, own_q if aligned else local_q, count)
    return pl.pallas_call(
        functools.partial(build_kernel, aligned=aligned),
        out_shape=pltpu.HBM((own_q // 2, 80, count), jnp.bfloat16),
        grid_spec=pltpu.PrefetchScalarGridSpec(
            num_scalar_prefetch=2,
            grid=(own_q // 2,),
            in_specs=[pl.BlockSpec(block, lambda i, first, _: (0, first[0] // own_q if aligned else 0, 0))],
            out_specs=pl.BlockSpec((1, 80, count), lambda i, *_: (i, 0, 0)),
        ),
        compiler_params=pltpu.CompilerParams(vmem_limit_bytes=16 << 20),
        cost_estimate=pl.CostEstimate(flops=4_000_000_000, bytes_accessed=4_000_000, transcendentals=0),
        name="build",
    )(first, lengths, pltpu.with_memory_space_constraint(points, pltpu.HBM))


def forward_kernel(first_ref, order_ref, length_ref, var_ref, weight_ref, rhs_ref, *rest, blocks, NB, SB):
    xy_refs, (out_ref, lhs_ref, acc) = rest[:blocks], rest[blocks:]
    local = 2 * pl.program_id(0)
    q = first_ref[0] + local
    points = rhs_ref.shape[2]
    part = xy_refs[0].shape[1]
    cells = blocks * part
    scale = scale_of(length_ref, q)
    u, w = (
        jnp.broadcast_to(jnp.concatenate([ref[d : d + 1, :] for ref in xy_refs], 1), (8, cells)) for d in (0, 1)
    )
    for k, rows in enumerate(cell_rows(u, w, scale)):
        lhs_ref[0, k] = rows.T.astype(jnp.bfloat16)

    def latent(k, _):
        for nb in range(cells // NB):
            rows = slice(nb * NB, (nb + 1) * NB)
            cell = lhs_ref[0, k, rows, :]
            total = jnp.zeros((NB, 128), jnp.float32)
            for j in range(points // SB):
                s = slice(j * SB, (j + 1) * SB)
                e = jnp.exp2(jnp.dot(cell, rhs_ref[0, :, s], preferred_element_type=jnp.float32))
                weight = weight_ref[pl.ds(q + k, 1), s]
                for c in range(SB // 128):
                    total = total + e[:, c * 128 : (c + 1) * 128] * weight[:, c * 128 : (c + 1) * 128]
            acc[rows, :] = total
        result = jnp.sum(acc[...].T, 0, keepdims=True) * var_ref[q + k]
        for b in range(blocks):
            for copy in range(out_ref.shape[0]):
                out_ref[copy, order_ref[b], pl.ds(local + k, 1), :] = result[:, b * part : (b + 1) * part]
        return 0

    for k in range(2):
        latent(k, 0)


def forward(first, order, lengths, var, weights, rhs, xys, own_q, copies):
    points = rhs.shape[2]
    blocks = len(xys)
    part = xys[0].shape[1]
    cells = blocks * part
    return pl.pallas_call(
        functools.partial(forward_kernel, blocks=blocks, NB=math.gcd(cells, 256), SB=points),
        grid=(own_q // 2,),
        out_shape=(
            jax.ShapeDtypeStruct((copies, blocks, own_q, part), jnp.float32),
            pltpu.HBM((own_q // 2, 2, cells, 80), jnp.bfloat16),
        ),
        in_specs=[whole(SMEM)] * 4
        + [whole(VMEM), pl.BlockSpec((1, 80, points), lambda i: (i, 0, 0))]
        + [whole(VMEM)] * blocks,
        out_specs=(whole(VMEM), pl.BlockSpec((1, 2, cells, 80), lambda i: (i, 0, 0, 0))),
        scratch_shapes=[VMEM((cells, 128), jnp.float32)],
        compiler_params=pltpu.CompilerParams(vmem_limit_bytes=ROOM),
        cost_estimate=pl.CostEstimate(flops=25_000_000_000, bytes_accessed=4_000_000, transcendentals=0),
        name="forward",
    )(first, order, lengths, var, weights, pltpu.with_memory_space_constraint(rhs, pltpu.HBM), *xys)


def backward_kernel(first_ref, order_ref, var_ref, grad_ref, rhs_ref, lhs_ref, out_ref, held, spread, *, NB, start):
    here = 2 * pl.program_id(0)
    local = 2 * start + here
    q = first_ref[0] + local
    points = rhs_ref.shape[2]
    copies, blocks, _, part = grad_ref.shape
    cells = blocks * part

    @pl.when(pl.program_id(0) == 0)
    def _():
        for b in range(blocks):
            held[b] = functools.reduce(jnp.add, [grad_ref[copy, order_ref[b]] for copy in range(copies)])

    def latent(k, _):
        for b in range(blocks):
            row = held[b, pl.ds(local + k, 1), :]
            spread[b * part : (b + 1) * part, :] = jnp.broadcast_to(row, (128, part)).T
        totals = [jnp.zeros((8, 128), jnp.float32) for _ in range(points // 128)]
        for nb in range(cells // NB):
            rows = slice(nb * NB, (nb + 1) * NB)
            cell = lhs_ref[0, k, rows, :]
            e = jnp.exp2(jnp.dot(cell, rhs_ref[0], preferred_element_type=jnp.float32))
            grad = spread[rows, :]
            for c in range(points // 128):
                term = (e[:, c * 128 : (c + 1) * 128] * grad).reshape(NB // 8, 8, 128)
                totals[c] = totals[c] + jnp.sum(term, 0)
        row = jnp.concatenate([jnp.sum(total, 0, keepdims=True) for total in totals], 1)
        out_ref[pl.ds(here + k, 1), :] = row * var_ref[q + k]
        return 0

    for k in range(2):
        latent(k, 0)


def backward(first, order, var, grads, rhs, lhs, start, pairs):
    points = rhs.shape[2]
    _, blocks, own_q, part = grads.shape
    cells = blocks * part
    return pl.pallas_call(
        functools.partial(backward_kernel, NB=math.gcd(cells, 256), start=start),
        grid=(pairs,),
        out_shape=jax.ShapeDtypeStruct((2 * pairs, points), jnp.float32),
        in_specs=[whole(SMEM)] * 3
        + [
            whole(VMEM),
            pl.BlockSpec((1, 80, points), lambda i: (i + start, 0, 0)),
            pl.BlockSpec((1, 2, cells, 80), lambda i: (i + start, 0, 0, 0)),
        ],
        out_specs=whole(VMEM),
        scratch_shapes=[VMEM((blocks, own_q, part), jnp.float32), VMEM((cells, 128), jnp.float32)],
        compiler_params=pltpu.CompilerParams(vmem_limit_bytes=ROOM),
        cost_estimate=pl.CostEstimate(flops=25_000_000_000, bytes_accessed=4_000_000, transcendentals=0),
        name="backward",
    )(first, order, var, grads, *(pltpu.with_memory_space_constraint(x, pltpu.HBM) for x in (rhs, lhs)))


def gather_kernel(order_ref, *refs):
    *piece_refs, out_ref = refs
    each = len(piece_refs) // order_ref.shape[0]
    for step in range(order_ref.shape[0]):
        rows = jnp.concatenate([ref[...] for ref in piece_refs[step * each : (step + 1) * each]], 0)
        out_ref[order_ref[step]] = rows


def gather(order, pieces):
    count = order.shape[0]
    rows = sum(piece.shape[0] for piece in pieces) // count
    width = pieces[0].shape[1]
    out = pl.pallas_call(
        gather_kernel,
        out_shape=jax.ShapeDtypeStruct((count, rows, width), jnp.float32),
        in_specs=[whole(SMEM)] + [whole(VMEM)] * len(pieces),
        out_specs=whole(VMEM),
        compiler_params=pltpu.CompilerParams(vmem_limit_bytes=16 << 20),
        name="gather",
    )(order, *pieces)
    return out.reshape(count * rows, width)


def observe_kernel(index_ref, expr_hbm, out_hbm, expr_ref, out_ref, load_sem, store_sem):
    rows, genes = expr_ref.shape
    count, cells, width = out_ref.shape
    columns = [slice(j * width, (j + 1) * width) for j in range(genes // width)]
    loads = [
        pltpu.make_async_copy(expr_hbm.at[:, s], expr_ref.at[:, s], load_sem.at[j]) for j, s in enumerate(columns)
    ]
    for copy in loads:
        copy.start()
    places = lax.broadcasted_iota(jnp.int32, (cells, rows), 1)
    hot = jnp.where(places == index_ref[...], 1.0, 0.0).astype(jnp.bfloat16)
    stores = []
    for j, s in enumerate(columns):
        loads[j].wait()
        out_ref[j] = jnp.dot(hot, expr_ref[:, s], preferred_element_type=jnp.float32).astype(jnp.bfloat16)
        copy = pltpu.make_async_copy(out_ref.at[j], out_hbm.at[j], store_sem.at[j])
        copy.start()
        stores.append(copy)
    for copy in stores:
        copy.wait()


def observe(index, expr):
    rows, genes = expr.shape
    cells = index.shape[0]
    width = math.gcd(genes, 512)
    count = genes // width
    return pl.pallas_call(
        observe_kernel,
        out_shape=pltpu.HBM((count, cells, width), jnp.bfloat16),
        in_specs=[whole(VMEM), whole(pltpu.HBM)],
        out_specs=whole(pltpu.HBM),
        scratch_shapes=[
            VMEM((rows, genes), jnp.bfloat16),
            VMEM((count, cells, width), jnp.bfloat16),
            pltpu.SemaphoreType.DMA((count,)),
            pltpu.SemaphoreType.DMA((count,)),
        ],
        compiler_params=pltpu.CompilerParams(vmem_limit_bytes=ROOM),
        cost_estimate=pl.CostEstimate(flops=3_000_000_000, bytes_accessed=6_000_000, transcendentals=0),
        name="observe",
    )(index[:, None], pltpu.with_memory_space_constraint(expr, pltpu.HBM))


def middle_kernel(rows_ref, piece_ref, mixing_ref, noise_ref, observed_ref, *rest, scale, cuts, shares):
    grad_refs, (send_ref, wide, latent) = rest[:shares], rest[shares:]
    latent_cuts, cell_cuts, lats, subs = cuts
    own_q, part = piece_ref.shape[2:]
    count, _, width = observed_ref.shape
    share = mixing_ref.shape[0] // shares
    for lat in range(lats):
        for a in range(latent_cuts):
            for b in range(cell_cuts):
                pieces = [piece_ref[a * cell_cuts + b, lat * subs + sub] for sub in range(subs)]
                first = (lat * latent_cuts + a) * own_q
                wide[first : first + own_q, b * part : (b + 1) * part] = functools.reduce(jnp.add, pieces)
    latent[...] = wide[...].astype(jnp.bfloat16)
    turned = wide[...].T.astype(jnp.bfloat16)
    halves = [latent[pl.ds(pl.multiple_of(rows_ref[i] * share, share), share), :] for i in range(shares)]
    ordered = jnp.concatenate(halves, 0)
    total = jnp.zeros(latent.shape, jnp.float32)
    for j in range(count):
        s = slice(j * width, (j + 1) * width)
        predicted = jnp.dot(turned, mixing_ref[:, s], preferred_element_type=jnp.float32)
        observed = observed_ref[j].astype(jnp.float32)
        weighted = (noise_ref[:, s] * (observed - predicted)).astype(jnp.bfloat16)
        grads = scale * jnp.dot(ordered, weighted, preferred_element_type=jnp.float32)
        for i in range(shares):
            grad_refs[i][:, s] = grads[i * share : (i + 1) * share]
        total = total + lax.dot_general(
            mixing_ref[:, s], weighted, (((1,), (1,)), ((), ())), preferred_element_type=jnp.float32
        )
    wide[...] = scale * total
    for lat in range(lats):
        for a in range(latent_cuts):
            for b in range(cell_cuts):
                first = (lat * latent_cuts + a) * own_q
                piece = wide[first : first + own_q, b * part : (b + 1) * part]
                for sub in range(subs):
                    send_ref[a * cell_cuts + b, lat * subs + sub] = piece


def middle(rows, pieces, mixing, noise, observed, scale, cuts):
    count, cells, width = observed.shape
    q, genes = mixing.shape
    shares = rows.shape[0]
    return pl.pallas_call(
        functools.partial(middle_kernel, scale=scale, cuts=cuts, shares=shares),
        out_shape=(jax.ShapeDtypeStruct((q // shares, genes), jnp.float32),) * shares
        + (jax.ShapeDtypeStruct(pieces.shape, jnp.float32),),
        in_specs=[whole(SMEM)] + [whole(VMEM)] * 4,
        out_specs=(whole(VMEM),) * (shares + 1),
        scratch_shapes=[
            VMEM((q, cells), jnp.float32),
            VMEM((q, cells), jnp.bfloat16),
        ],
        compiler_params=pltpu.CompilerParams(vmem_limit_bytes=ROOM),
        cost_estimate=pl.CostEstimate(flops=3_000_000_000, bytes_accessed=4_000_000, transcendentals=0),
        name="middle",
    )(
        rows,
        pieces,
        mixing,
        noise[None, :],
        observed,
    )


def shifted(x, axes, step, size):
    return lax.ppermute(x, axes, [(partner(i, step, size), i) for i in range(size)])


def gather_rows(x, axis):
    n = lax.axis_size(axis)
    me = lax.axis_index(axis)
    rows = x.shape[0]
    out = lax.dynamic_update_slice_in_dim(jnp.zeros((n * rows, x.shape[1]), x.dtype), x, me * rows, 0)
    for step in range(1, n):
        out = lax.dynamic_update_slice_in_dim(out, shifted(x, axis, step, n), partner(me, step, n) * rows, 0)
    return out


def on_device(cell_index, coords_table, expr_table, inducing, ind_weights, lengthscale, variance, mixing, noise_prec):
    genes, lats, subs = (lax.axis_size(name) for name in ("gene", "lat", "sub"))
    blocks = lats * subs
    cells = cell_index.shape[0]
    local_q, points = ind_weights.shape
    latent_cuts = math.gcd(genes, local_q // 2)
    cell_cuts = genes // latent_cuts
    cuts = (latent_cuts, cell_cuts, lats, subs)
    own_q = local_q // latent_cuts
    part = cells // cell_cuts
    place = lax.axis_index("gene")
    block = lax.axis_index("lat") * subs + lax.axis_index("sub")
    first = (place // cell_cuts * own_q).reshape(1)
    order = jnp.stack([partner(block, step, blocks) for step in range(blocks)])
    every = ("gene", "lat", "sub")

    local_xy = locate(cell_index, coords_table)
    xys = [local_xy] + [shifted(local_xy, ("lat", "sub"), step, blocks) for step in range(1, blocks)]
    xys = [lax.dynamic_slice_in_dim(xy, place % cell_cuts * part, part, 1) for xy in xys]
    rhs = build(first, lengthscale, inducing, own_q)

    partial, lhs = forward(first, order, lengthscale, variance, ind_weights, rhs, xys, own_q, genes)
    late_index, partial = lax.optimization_barrier((cell_index, partial))
    pieces = lax.all_to_all(partial.reshape(genes * blocks, own_q, part), every, 0, 0, tiled=True)
    observed = observe(late_index, expr_table)

    grad_scale = -1.0 / math.sqrt(cells * blocks)
    sub = lax.axis_index("sub")
    rows = [sub ^ step if subs & (subs - 1) == 0 else (sub - step) % subs for step in range(subs)]
    *terms, send = middle(
        jnp.stack(rows), pieces.reshape(genes, blocks, own_q, part), mixing, noise_prec, observed, grad_scale, cuts
    )
    pieces = lax.all_to_all(send.reshape(genes * blocks, own_q, part), every, 0, 0, tiled=True)
    half = functools.reduce(
        jnp.add, [terms[0]] + [shifted(terms[step], "sub", step, subs) for step in range(1, subs)]
    )
    others = [shifted(half, "lat", step, lats) for step in range(1, lats)]

    grads = pieces.reshape(genes, blocks, own_q, part)
    pairs = own_q // 2
    early = pairs // 2 if cell_cuts == 1 else 0
    cut = [(0, early), (early, pairs)] if early else [(0, pairs)]
    inducing_terms, arrived = [], []
    for start, stop in cut:
        term = backward(first, order, variance, grads, rhs, lhs, start, stop - start)
        if start == 0:
            term, *others = lax.optimization_barrier((term, *others))
            half = functools.reduce(jnp.add, others, half)
        else:
            term, arrived = lax.optimization_barrier((term, arrived))
        inducing_terms.append(term)
        if cell_cuts == 1:
            arrived = arrived + [[shifted(term, "gene", step, genes) for step in range(1, genes)]]
    grad_mixing = gather_rows(half, "sub")
    if cell_cuts == 1:
        gene_order = jnp.stack([partner(place, step, genes) for step in range(genes)])
        pieces = list(inducing_terms)
        for step in range(genes - 1):
            pieces += [parts[step] for parts in arrived]
        return (grad_mixing, gather(gene_order, pieces))
    gathered = lax.all_gather(inducing_terms[0], "gene", axis=0, tiled=True)
    grad_inducing = gathered.reshape(latent_cuts, cell_cuts, own_q, points).sum(1)
    return (grad_mixing, grad_inducing.reshape(local_q, points))


def solution(mesh):
    in_specs = (
        P(("group", "lat", "sub")),
        P("group", ("lat", "sub")),
        P(("group", "lat", "sub"), "gene"),
        P("group", "lat", "sub"),
        P(("group", "lat"), "sub"),
        P(("group", "lat")),
        P(("group", "lat")),
        P("group", "gene"),
        P(("group", "gene")),
    )
    out_specs = (P("group", "gene"), P(("group", "lat"), "sub"))
    return jax.shard_map(
        on_device, mesh=mesh, in_specs=in_specs, out_specs=out_specs, check_vma=False
    )
```

```python
import functools
import math

import jax
import jax.numpy as jnp
from jax import lax
from jax.experimental import pallas as pl
from jax.experimental.pallas import tpu as pltpu
from jax.sharding import PartitionSpec as P

LOG2E = math.log2(math.e)
ROOM = 24 << 20

def row_of(shape):
    return lax.broadcasted_iota(jnp.int32, shape, 0)

def parts(u, w, a):
    L = u.shape[1]
    U = (u - 0.5) * a
    W = (w - 0.5) * a
    big = 1.5 * 2.0**20
    U1 = (U + big) - big
    W1 = (W + big) - big
    rU = U - U1
    rW = W - W1
    hi = U1 * U1 + W1 * W1
    lo = rU * (U1 + U) + rW * (W1 + W)
    r = row_of((8, L)) % 4
    T = jnp.where(r == 0, U, jnp.where(r == 1, W, jnp.where(r == 2, hi, lo)))
    rc = row_of((8, 1)) % 4
    magic = jnp.where(rc <= 1, 1.5 * 2.0**20, jnp.where(rc == 2, 1.5 * 2.0**26, 1.5 * 2.0**18)).astype(jnp.float32)
    T1 = ((T + magic) - magic).astype(jnp.bfloat16).astype(jnp.float32)
    R = T - T1
    T2 = R.astype(jnp.bfloat16).astype(jnp.float32)
    T3 = R - T2
    return T1, T2, T3

def point_rows(u, w, a):
    T1, T2, T3 = parts(u, w, a)
    one = jnp.ones_like(T1)
    return jnp.concatenate([T1, T1, T2, T2, T1, T2, T3, T3, one, jnp.zeros_like(one)], 0).astype(jnp.bfloat16)

def cell_rows(u, w, a):
    T1, T2, T3 = parts(u, w, a)
    r8 = row_of(T1.shape)
    r = r8 % 4
    xy = r <= 1
    A1 = jnp.where(xy, 2 * T1, -1.0)
    A2 = jnp.where(xy, 2 * T2, 0.0)
    A3 = jnp.where(xy, 2 * T3, 0.0)
    outs = []
    for k in range(2):
        mine = (r8 // 4) == k
        G = [jnp.where(mine, A, 0.0) for A in (A1, A2, A3)]
        def n(T, i):
            return -T[4 * k + i : 4 * k + i + 1]
        z = jnp.zeros_like(n(T1, 0))
        norm = jnp.concatenate([n(T1, 2), n(T2, 2), n(T1, 3), n(T2, 3), n(T3, 3), z, z, z], 0)
        G1, G2, G3 = G
        outs.append(jnp.concatenate([G1, G2, G1, G2, G3, G3, G1, G2, norm, jnp.zeros_like(norm)], 0))
    return outs

VMEM = pltpu.VMEM
SMEM = pltpu.SMEM


def whole(space):
    return pl.BlockSpec(memory_space=space)


def partner(place, step, blocks):
    if blocks & (blocks - 1) == 0:
        return place ^ step
    return (place + step) % blocks


def locate_kernel(index_ref, table_ref, out_ref):
    table = table_ref[...]
    rows = table.shape[1]
    column = jnp.concatenate([table, jnp.zeros((8 - table.shape[0], rows), jnp.float32)], 0).T
    hot = lax.broadcasted_iota(jnp.int32, (rows, index_ref.shape[1]), 0) == index_ref[...]
    picked = [
        jnp.sum(jnp.where(hot, column[:, axis : axis + 1], 0.0), 0, keepdims=True)
        for axis in range(table.shape[0])
    ]
    out_ref[...] = jnp.concatenate(picked, 0)


def locate(index, table):
    return pl.pallas_call(
        locate_kernel,
        out_shape=jax.ShapeDtypeStruct((table.shape[0], index.shape[0]), jnp.float32),
        name="locate",
    )(index[None, :], table)


def scale_of(length_ref, q):
    lengths = jnp.where(row_of((8, 1)) < 4, length_ref[q], length_ref[q + 1])
    return math.sqrt(0.5 * LOG2E) / lengths


def build_kernel(first_ref, length_ref, points_ref, rhs_ref, *, aligned):
    local = 2 * pl.program_id(0)
    scale = scale_of(length_ref, first_ref[0] + local)
    row = local if aligned else first_ref[0] + local
    width = points_ref.shape[2]

    def step(i, _):
        s = pl.ds(pl.multiple_of(i * width, width), width)
        low = row_of((8, width)) < 4
        u, w = (
            jnp.where(low, points_ref[d, pl.ds(row, 1), s], points_ref[d, pl.ds(row + 1, 1), s]) for d in (0, 1)
        )
        rhs_ref[0, :, s] = point_rows(u, w, scale)
        return 0

    lax.fori_loop(0, points_ref.shape[2] // width, step, 0)


def build(first, lengths, points, own_q):
    axes, local_q, count = points.shape
    aligned = own_q % 8 == 0
    block = (axes, own_q if aligned else local_q, count)
    return pl.pallas_call(
        functools.partial(build_kernel, aligned=aligned),
        out_shape=pltpu.HBM((own_q // 2, 80, count), jnp.bfloat16),
        grid_spec=pltpu.PrefetchScalarGridSpec(
            num_scalar_prefetch=2,
            grid=(own_q // 2,),
            in_specs=[pl.BlockSpec(block, lambda i, first, _: (0, first[0] // own_q if aligned else 0, 0))],
            out_specs=pl.BlockSpec((1, 80, count), lambda i, *_: (i, 0, 0)),
        ),
        compiler_params=pltpu.CompilerParams(vmem_limit_bytes=16 << 20),
        cost_estimate=pl.CostEstimate(flops=4_000_000_000, bytes_accessed=4_000_000, transcendentals=0),
        name="build",
    )(first, pltpu.with_memory_space_constraint(lengths, pltpu.HBM), pltpu.with_memory_space_constraint(points, pltpu.HBM))


def forward_kernel(first_ref, order_ref, length_ref, var_ref, weight_ref, rhs_ref, *rest, blocks, NB, SB):
    xy_refs, (out_ref, lhs_ref, acc) = rest[:blocks], rest[blocks:]
    local = 2 * pl.program_id(0)
    q = first_ref[0] + local
    points = rhs_ref.shape[2]
    part = xy_refs[0].shape[1]
    cells = blocks * part
    scale = scale_of(length_ref, q)
    u, w = (
        jnp.broadcast_to(jnp.concatenate([ref[d : d + 1, :] for ref in xy_refs], 1), (8, cells)) for d in (0, 1)
    )
    for k, rows in enumerate(cell_rows(u, w, scale)):
        lhs_ref[0, k] = rows.T.astype(jnp.bfloat16)

    def latent(k, _):
        for nb in range(cells // NB):
            rows = slice(nb * NB, (nb + 1) * NB)
            cell = lhs_ref[0, k, rows, :]
            total = jnp.zeros((NB, 128), jnp.float32)
            for j in range(points // SB):
                s = slice(j * SB, (j + 1) * SB)
                e = jnp.exp2(jnp.dot(cell, rhs_ref[0, :, s], preferred_element_type=jnp.float32))
                weight = weight_ref[pl.ds(q + k, 1), s]
                for c in range(SB // 128):
                    total = total + e[:, c * 128 : (c + 1) * 128] * weight[:, c * 128 : (c + 1) * 128]
            acc[rows, :] = total
        result = jnp.sum(acc[...].T, 0, keepdims=True) * var_ref[q + k]
        for b in range(blocks):
            for copy in range(out_ref.shape[0]):
                out_ref[copy, order_ref[b], pl.ds(local + k, 1), :] = result[:, b * part : (b + 1) * part]
        return 0

    for k in range(2):
        latent(k, 0)


def forward(first, order, lengths, var, weights, rhs, xys, own_q, copies):
    points = rhs.shape[2]
    blocks = len(xys)
    part = xys[0].shape[1]
    cells = blocks * part
    return pl.pallas_call(
        functools.partial(forward_kernel, blocks=blocks, NB=math.gcd(cells, 256), SB=points),
        grid=(own_q // 2,),
        out_shape=(
            jax.ShapeDtypeStruct((copies, blocks, own_q, part), jnp.float32),
            pltpu.HBM((own_q // 2, 2, cells, 80), jnp.bfloat16),
        ),
        in_specs=[whole(SMEM)] * 4
        + [whole(VMEM), pl.BlockSpec((1, 80, points), lambda i: (i, 0, 0))]
        + [whole(VMEM)] * blocks,
        out_specs=(whole(VMEM), pl.BlockSpec((1, 2, cells, 80), lambda i: (i, 0, 0, 0))),
        scratch_shapes=[VMEM((cells, 128), jnp.float32)],
        compiler_params=pltpu.CompilerParams(vmem_limit_bytes=ROOM),
        cost_estimate=pl.CostEstimate(flops=25_000_000_000, bytes_accessed=4_000_000, transcendentals=0),
        name="forward",
    )(first, order, lengths, var, weights, pltpu.with_memory_space_constraint(rhs, pltpu.HBM), *xys)


def backward_kernel(first_ref, order_ref, var_ref, grad_ref, rhs_ref, lhs_ref, out_ref, held, spread, *, NB, start):
    here = 2 * pl.program_id(0)
    local = 2 * start + here
    q = first_ref[0] + local
    points = rhs_ref.shape[2]
    copies, blocks, _, part = grad_ref.shape
    cells = blocks * part

    @pl.when(pl.program_id(0) == 0)
    def _():
        for b in range(blocks):
            held[b] = functools.reduce(jnp.add, [grad_ref[copy, order_ref[b]] for copy in range(copies)])

    def latent(k, _):
        for b in range(blocks):
            row = held[b, pl.ds(local + k, 1), :]
            spread[b * part : (b + 1) * part, :] = jnp.broadcast_to(row, (128, part)).T
        totals = [jnp.zeros((8, 128), jnp.float32) for _ in range(points // 128)]
        for nb in range(cells // NB):
            rows = slice(nb * NB, (nb + 1) * NB)
            cell = lhs_ref[0, k, rows, :]
            e = jnp.exp2(jnp.dot(cell, rhs_ref[0], preferred_element_type=jnp.float32))
            grad = spread[rows, :]
            for c in range(points // 128):
                term = (e[:, c * 128 : (c + 1) * 128] * grad).reshape(NB // 8, 8, 128)
                totals[c] = totals[c] + jnp.sum(term, 0)
        row = jnp.concatenate([jnp.sum(total, 0, keepdims=True) for total in totals], 1)
        out_ref[pl.ds(here + k, 1), :] = row * var_ref[q + k]
        return 0

    for k in range(2):
        latent(k, 0)


def backward(first, order, var, grads, rhs, lhs, start, pairs):
    points = rhs.shape[2]
    _, blocks, own_q, part = grads.shape
    cells = blocks * part
    return pl.pallas_call(
        functools.partial(backward_kernel, NB=math.gcd(cells, 256), start=start),
        grid=(pairs,),
        out_shape=jax.ShapeDtypeStruct((2 * pairs, points), jnp.float32),
        in_specs=[whole(SMEM)] * 3
        + [
            whole(VMEM),
            pl.BlockSpec((1, 80, points), lambda i: (i + start, 0, 0)),
            pl.BlockSpec((1, 2, cells, 80), lambda i: (i + start, 0, 0, 0)),
        ],
        out_specs=whole(VMEM),
        scratch_shapes=[VMEM((blocks, own_q, part), jnp.float32), VMEM((cells, 128), jnp.float32)],
        compiler_params=pltpu.CompilerParams(vmem_limit_bytes=ROOM),
        cost_estimate=pl.CostEstimate(flops=25_000_000_000, bytes_accessed=4_000_000, transcendentals=0),
        name="backward",
    )(first, order, var, grads, *(pltpu.with_memory_space_constraint(x, pltpu.HBM) for x in (rhs, lhs)))


def gather_kernel(order_ref, *refs):
    *piece_refs, out_ref = refs
    each = len(piece_refs) // order_ref.shape[0]
    for step in range(order_ref.shape[0]):
        rows = jnp.concatenate([ref[...] for ref in piece_refs[step * each : (step + 1) * each]], 0)
        out_ref[order_ref[step]] = rows


def gather(order, pieces):
    count = order.shape[0]
    rows = sum(piece.shape[0] for piece in pieces) // count
    width = pieces[0].shape[1]
    out = pl.pallas_call(
        gather_kernel,
        out_shape=jax.ShapeDtypeStruct((count, rows, width), jnp.float32),
        in_specs=[whole(SMEM)] + [whole(VMEM)] * len(pieces),
        out_specs=whole(VMEM),
        compiler_params=pltpu.CompilerParams(vmem_limit_bytes=16 << 20),
        cost_estimate=pl.CostEstimate(flops=0, bytes_accessed=2_000_000, transcendentals=0),
        name="gather",
    )(order, *pieces)
    return out.reshape(count * rows, width)


def observe_kernel(index_ref, expr_hbm, out_hbm, expr_ref, out_ref, load_sem, store_sem):
    rows, genes = expr_ref.shape
    count, cells, width = out_ref.shape
    columns = [slice(j * width, (j + 1) * width) for j in range(genes // width)]
    loads = [
        pltpu.make_async_copy(expr_hbm.at[:, s], expr_ref.at[:, s], load_sem.at[j]) for j, s in enumerate(columns)
    ]
    for copy in loads:
        copy.start()
    places = lax.broadcasted_iota(jnp.int32, (cells, rows), 1)
    hot = jnp.where(places == index_ref[...], 1.0, 0.0).astype(jnp.bfloat16)
    stores = []
    for j, s in enumerate(columns):
        loads[j].wait()
        out_ref[j] = jnp.dot(hot, expr_ref[:, s], preferred_element_type=jnp.float32).astype(jnp.bfloat16)
        copy = pltpu.make_async_copy(out_ref.at[j], out_hbm.at[j], store_sem.at[j])
        copy.start()
        stores.append(copy)
    for copy in stores:
        copy.wait()


def observe(index, expr):
    rows, genes = expr.shape
    cells = index.shape[0]
    width = math.gcd(genes, 1024)
    count = genes // width
    return pl.pallas_call(
        observe_kernel,
        out_shape=pltpu.HBM((count, cells, width), jnp.bfloat16),
        in_specs=[whole(VMEM), whole(pltpu.HBM)],
        out_specs=whole(pltpu.HBM),
        scratch_shapes=[
            VMEM((rows, genes), jnp.bfloat16),
            VMEM((count, cells, width), jnp.bfloat16),
            pltpu.SemaphoreType.DMA((count,)),
            pltpu.SemaphoreType.DMA((count,)),
        ],
        compiler_params=pltpu.CompilerParams(vmem_limit_bytes=ROOM),
        cost_estimate=pl.CostEstimate(flops=3_000_000_000, bytes_accessed=6_000_000, transcendentals=0),
        name="observe",
    )(index[:, None], pltpu.with_memory_space_constraint(expr, pltpu.HBM))


def middle_kernel(rows_ref, piece_ref, mixing_ref, noise_ref, observed_ref, *rest, scale, cuts, shares):
    grad_refs, (send_ref, wide, latent) = rest[:shares], rest[shares:]
    latent_cuts, cell_cuts, lats, subs = cuts
    own_q, part = piece_ref.shape[2:]
    count, _, width = observed_ref.shape
    share = mixing_ref.shape[0] // shares
    for lat in range(lats):
        for a in range(latent_cuts):
            for b in range(cell_cuts):
                pieces = [piece_ref[a * cell_cuts + b, lat * subs + sub] for sub in range(subs)]
                first = (lat * latent_cuts + a) * own_q
                wide[first : first + own_q, b * part : (b + 1) * part] = functools.reduce(jnp.add, pieces)
    latent[...] = wide[...].astype(jnp.bfloat16)
    turned = wide[...].T.astype(jnp.bfloat16)
    halves = [latent[pl.ds(pl.multiple_of(rows_ref[i] * share, share), share), :] for i in range(shares)]
    ordered = jnp.concatenate(halves, 0)
    total = jnp.zeros(latent.shape, jnp.float32)
    for j in range(count):
        s = slice(j * width, (j + 1) * width)
        predicted = jnp.dot(turned, mixing_ref[:, s], preferred_element_type=jnp.float32)
        observed = observed_ref[j].astype(jnp.float32)
        weighted = (noise_ref[:, s] * (observed - predicted)).astype(jnp.bfloat16)
        grads = scale * jnp.dot(ordered, weighted, preferred_element_type=jnp.float32)
        for i in range(shares):
            grad_refs[i][:, s] = grads[i * share : (i + 1) * share]
        total = total + lax.dot_general(
            mixing_ref[:, s], weighted, (((1,), (1,)), ((), ())), preferred_element_type=jnp.float32
        )
    wide[...] = scale * total
    for lat in range(lats):
        for a in range(latent_cuts):
            for b in range(cell_cuts):
                first = (lat * latent_cuts + a) * own_q
                piece = wide[first : first + own_q, b * part : (b + 1) * part]
                for sub in range(subs):
                    send_ref[a * cell_cuts + b, lat * subs + sub] = piece


def middle(rows, pieces, mixing, noise, observed, scale, cuts):
    count, cells, width = observed.shape
    q, genes = mixing.shape
    shares = rows.shape[0]
    return pl.pallas_call(
        functools.partial(middle_kernel, scale=scale, cuts=cuts, shares=shares),
        out_shape=(jax.ShapeDtypeStruct((q // shares, genes), jnp.float32),) * shares
        + (jax.ShapeDtypeStruct(pieces.shape, jnp.float32),),
        in_specs=[whole(SMEM)] + [whole(VMEM)] * 4,
        out_specs=(whole(VMEM),) * (shares + 1),
        scratch_shapes=[
            VMEM((q, cells), jnp.float32),
            VMEM((q, cells), jnp.bfloat16),
        ],
        compiler_params=pltpu.CompilerParams(vmem_limit_bytes=ROOM),
        cost_estimate=pl.CostEstimate(flops=3_000_000_000, bytes_accessed=4_000_000, transcendentals=0),
        name="middle",
    )(
        rows,
        pieces,
        mixing,
        noise[None, :],
        observed,
    )


def shifted(x, axes, step, size):
    return lax.ppermute(x, axes, [(partner(i, step, size), i) for i in range(size)])


def on_device(cell_index, coords_table, expr_table, inducing, ind_weights, lengthscale, variance, mixing, noise_prec):
    genes, lats, subs = (lax.axis_size(name) for name in ("gene", "lat", "sub"))
    blocks = lats * subs
    cells = cell_index.shape[0]
    local_q, points = ind_weights.shape
    latent_cuts = math.gcd(genes, local_q // 2)
    cell_cuts = genes // latent_cuts
    cuts = (latent_cuts, cell_cuts, lats, subs)
    own_q = local_q // latent_cuts
    part = cells // cell_cuts
    place = lax.axis_index("gene")
    block = lax.axis_index("lat") * subs + lax.axis_index("sub")
    first = (place // cell_cuts * own_q).reshape(1)
    order = jnp.stack([partner(block, step, blocks) for step in range(blocks)])
    every = ("gene", "lat", "sub")

    local_xy = locate(cell_index, coords_table)
    xys = [local_xy] + [shifted(local_xy, ("lat", "sub"), step, blocks) for step in range(1, blocks)]
    xys = [lax.dynamic_slice_in_dim(xy, place % cell_cuts * part, part, 1) for xy in xys]
    rhs = build(first, lengthscale, inducing, own_q)

    partial, lhs = forward(first, order, lengthscale, variance, ind_weights, rhs, xys, own_q, genes)
    late_index, partial = lax.optimization_barrier((cell_index, partial))
    pieces = lax.all_to_all(partial.reshape(genes * blocks, own_q, part), every, 0, 0, tiled=True)
    observed = observe(late_index, expr_table)

    grad_scale = -1.0 / math.sqrt(cells * blocks)
    sub = lax.axis_index("sub")
    rows = [sub ^ step if subs & (subs - 1) == 0 else (sub - step) % subs for step in range(subs)]
    *terms, send = middle(
        jnp.stack(rows), pieces.reshape(genes, blocks, own_q, part), mixing, noise_prec, observed, grad_scale, cuts
    )
    pieces = lax.all_to_all(send.reshape(genes * blocks, own_q, part), every, 0, 0, tiled=True)
    half = functools.reduce(
        jnp.add, [terms[0]] + [shifted(terms[step], "sub", step, subs) for step in range(1, subs)]
    )
    others = [shifted(half, "lat", step, lats) for step in range(1, lats)]

    grads = pieces.reshape(genes, blocks, own_q, part)
    pairs = own_q // 2
    early = pairs // 2 if cell_cuts == 1 else 0
    cut = [(0, early), (early, pairs)] if early else [(0, pairs)]
    inducing_terms, arrived = [], []
    for start, stop in cut:
        term = backward(first, order, variance, grads, rhs, lhs, start, stop - start)
        if start == 0:
            term, *others = lax.optimization_barrier((term, *others))
            half = functools.reduce(jnp.add, others, half)
        else:
            term, arrived = lax.optimization_barrier((term, arrived))
        inducing_terms.append(term)
        if cell_cuts == 1:
            arrived = arrived + [[shifted(term, "gene", step, genes) for step in range(1, genes)]]
    sub_order = jnp.stack([partner(sub, step, subs) for step in range(subs)])
    grad_mixing = gather(sub_order, [half] + [shifted(half, "sub", step, subs) for step in range(1, subs)])
    if cell_cuts == 1:
        gene_order = jnp.stack([partner(place, step, genes) for step in range(genes)])
        pieces = list(inducing_terms)
        for step in range(genes - 1):
            pieces += [parts[step] for parts in arrived]
        pieces, grad_mixing = lax.optimization_barrier((pieces, grad_mixing))
        return (grad_mixing, gather(gene_order, pieces))
    gathered = lax.all_gather(inducing_terms[0], "gene", axis=0, tiled=True)
    grad_inducing = gathered.reshape(latent_cuts, cell_cuts, own_q, points).sum(1)
    return (grad_mixing, grad_inducing.reshape(local_q, points))


def solution(mesh):
    in_specs = (
        P(("group", "lat", "sub")),
        P("group", ("lat", "sub")),
        P(("group", "lat", "sub"), "gene"),
        P("group", "lat", "sub"),
        P(("group", "lat"), "sub"),
        P(("group", "lat")),
        P(("group", "lat")),
        P("group", "gene"),
        P(("group", "gene")),
    )
    out_specs = (P("group", "gene"), P(("group", "lat"), "sub"))
    return jax.shard_map(
        on_device, mesh=mesh, in_specs=in_specs, out_specs=out_specs, check_vma=False
    )
```

```python
import functools
import math

import jax
import jax.numpy as jnp
from jax import lax
from jax.experimental import pallas as pl
from jax.experimental.pallas import tpu as pltpu
from jax.sharding import PartitionSpec as P

LOG2E = math.log2(math.e)
ROOM = 24 << 20

def row_of(shape):
    return lax.broadcasted_iota(jnp.int32, shape, 0)

def parts(u, w, a):
    L = u.shape[1]
    U = (u - 0.5) * a
    W = (w - 0.5) * a
    big = 1.5 * 2.0**20
    U1 = (U + big) - big
    W1 = (W + big) - big
    rU = U - U1
    rW = W - W1
    hi = U1 * U1 + W1 * W1
    lo = rU * (U1 + U) + rW * (W1 + W)
    r = row_of((8, L)) % 4
    T = jnp.where(r == 0, U, jnp.where(r == 1, W, jnp.where(r == 2, hi, lo)))
    rc = row_of((8, 1)) % 4
    magic = jnp.where(rc <= 1, 1.5 * 2.0**20, jnp.where(rc == 2, 1.5 * 2.0**26, 1.5 * 2.0**18)).astype(jnp.float32)
    T1 = ((T + magic) - magic).astype(jnp.bfloat16).astype(jnp.float32)
    R = T - T1
    T2 = R.astype(jnp.bfloat16).astype(jnp.float32)
    T3 = R - T2
    return T1, T2, T3

def point_rows(u, w, a):
    T1, T2, T3 = parts(u, w, a)
    one = jnp.ones_like(T1)
    return jnp.concatenate([T1, T1, T2, T2, T1, T2, T3, T3, one, jnp.zeros_like(one)], 0).astype(jnp.bfloat16)

def cell_rows(u, w, a):
    T1, T2, T3 = parts(u, w, a)
    r8 = row_of(T1.shape)
    r = r8 % 4
    xy = r <= 1
    A1 = jnp.where(xy, 2 * T1, -1.0)
    A2 = jnp.where(xy, 2 * T2, 0.0)
    A3 = jnp.where(xy, 2 * T3, 0.0)
    outs = []
    for k in range(2):
        mine = (r8 // 4) == k
        G = [jnp.where(mine, A, 0.0) for A in (A1, A2, A3)]
        def n(T, i):
            return -T[4 * k + i : 4 * k + i + 1]
        z = jnp.zeros_like(n(T1, 0))
        norm = jnp.concatenate([n(T1, 2), n(T2, 2), n(T1, 3), n(T2, 3), n(T3, 3), z, z, z], 0)
        G1, G2, G3 = G
        outs.append(jnp.concatenate([G1, G2, G1, G2, G3, G3, G1, G2, norm, jnp.zeros_like(norm)], 0))
    return outs

VMEM = pltpu.VMEM
SMEM = pltpu.SMEM


def whole(space):
    return pl.BlockSpec(memory_space=space)


def partner(place, step, blocks):
    if blocks & (blocks - 1) == 0:
        return place ^ step
    return (place + step) % blocks


def locate_kernel(index_ref, table_ref, out_ref):
    table = table_ref[...]
    rows = table.shape[1]
    column = jnp.concatenate([table, jnp.zeros((8 - table.shape[0], rows), jnp.float32)], 0).T
    hot = lax.broadcasted_iota(jnp.int32, (rows, index_ref.shape[1]), 0) == index_ref[...]
    picked = [
        jnp.sum(jnp.where(hot, column[:, axis : axis + 1], 0.0), 0, keepdims=True)
        for axis in range(table.shape[0])
    ]
    out_ref[...] = jnp.concatenate(picked, 0)


def locate(index, table):
    return pl.pallas_call(
        locate_kernel,
        out_shape=jax.ShapeDtypeStruct((table.shape[0], index.shape[0]), jnp.float32),
        name="locate",
    )(index[None, :], table)


def scale_of(length_ref, q):
    lengths = jnp.where(row_of((8, 1)) < 4, length_ref[q], length_ref[q + 1])
    return math.sqrt(0.5 * LOG2E) / lengths


def build_kernel(first_ref, length_ref, points_ref, rhs_ref, *, aligned):
    local = 2 * pl.program_id(0)
    scale = scale_of(length_ref, first_ref[0] + local)
    row = local if aligned else first_ref[0] + local
    width = points_ref.shape[2]

    def step(i, _):
        s = pl.ds(pl.multiple_of(i * width, width), width)
        low = row_of((8, width)) < 4
        u, w = (
            jnp.where(low, points_ref[d, pl.ds(row, 1), s], points_ref[d, pl.ds(row + 1, 1), s]) for d in (0, 1)
        )
        rhs_ref[0, :, s] = point_rows(u, w, scale)
        return 0

    lax.fori_loop(0, points_ref.shape[2] // width, step, 0)


def build(first, lengths, points, own_q):
    axes, local_q, count = points.shape
    aligned = own_q % 8 == 0
    block = (axes, own_q if aligned else local_q, count)
    return pl.pallas_call(
        functools.partial(build_kernel, aligned=aligned),
        out_shape=pltpu.HBM((own_q // 2, 80, count), jnp.bfloat16),
        grid_spec=pltpu.PrefetchScalarGridSpec(
            num_scalar_prefetch=2,
            grid=(own_q // 2,),
            in_specs=[pl.BlockSpec(block, lambda i, first, _: (0, first[0] // own_q if aligned else 0, 0))],
            out_specs=pl.BlockSpec((1, 80, count), lambda i, *_: (i, 0, 0)),
        ),
        compiler_params=pltpu.CompilerParams(vmem_limit_bytes=16 << 20),
        cost_estimate=pl.CostEstimate(flops=4_000_000_000, bytes_accessed=4_000_000, transcendentals=0),
        name="build",
    )(first, pltpu.with_memory_space_constraint(lengths, pltpu.HBM), pltpu.with_memory_space_constraint(points, pltpu.HBM))


def forward_kernel(first_ref, order_ref, length_ref, var_ref, weight_ref, rhs_ref, *rest, blocks, NB, SB):
    xy_refs, (out_ref, lhs_ref, acc) = rest[:blocks], rest[blocks:]
    local = 2 * pl.program_id(0)
    q = first_ref[0] + local
    points = rhs_ref.shape[2]
    part = xy_refs[0].shape[1]
    cells = blocks * part
    scale = scale_of(length_ref, q)
    u, w = (
        jnp.broadcast_to(jnp.concatenate([ref[d : d + 1, :] for ref in xy_refs], 1), (8, cells)) for d in (0, 1)
    )
    for k, rows in enumerate(cell_rows(u, w, scale)):
        lhs_ref[0, k] = rows.T.astype(jnp.bfloat16)

    def latent(k, _):
        for nb in range(cells // NB):
            rows = slice(nb * NB, (nb + 1) * NB)
            cell = lhs_ref[0, k, rows, :]
            total = jnp.zeros((NB, 128), jnp.float32)
            for j in range(points // SB):
                s = slice(j * SB, (j + 1) * SB)
                e = jnp.exp2(jnp.dot(cell, rhs_ref[0, :, s], preferred_element_type=jnp.float32))
                weight = weight_ref[pl.ds(q + k, 1), s]
                for c in range(SB // 128):
                    total = total + e[:, c * 128 : (c + 1) * 128] * weight[:, c * 128 : (c + 1) * 128]
            acc[rows, :] = total
        result = jnp.sum(acc[...].T, 0, keepdims=True) * var_ref[q + k]
        for b in range(blocks):
            for copy in range(out_ref.shape[0]):
                out_ref[copy, order_ref[b], pl.ds(local + k, 1), :] = result[:, b * part : (b + 1) * part]
        return 0

    for k in range(2):
        latent(k, 0)


def forward(first, order, lengths, var, weights, rhs, xys, own_q, copies):
    points = rhs.shape[2]
    blocks = len(xys)
    part = xys[0].shape[1]
    cells = blocks * part
    return pl.pallas_call(
        functools.partial(forward_kernel, blocks=blocks, NB=math.gcd(cells, 256), SB=points),
        grid=(own_q // 2,),
        out_shape=(
            jax.ShapeDtypeStruct((copies, blocks, own_q, part), jnp.float32),
            pltpu.HBM((own_q // 2, 2, cells, 80), jnp.bfloat16),
        ),
        in_specs=[whole(SMEM)] * 4
        + [whole(VMEM), pl.BlockSpec((1, 80, points), lambda i: (i, 0, 0))]
        + [whole(VMEM)] * blocks,
        out_specs=(whole(VMEM), pl.BlockSpec((1, 2, cells, 80), lambda i: (i, 0, 0, 0))),
        scratch_shapes=[VMEM((cells, 128), jnp.float32)],
        compiler_params=pltpu.CompilerParams(vmem_limit_bytes=ROOM),
        cost_estimate=pl.CostEstimate(flops=25_000_000_000, bytes_accessed=4_000_000, transcendentals=0),
        name="forward",
    )(first, order, lengths, var, weights, pltpu.with_memory_space_constraint(rhs, pltpu.HBM), *xys)


def backward_kernel(first_ref, order_ref, var_ref, grad_ref, rhs_ref, lhs_ref, out_ref, held, spread, *, NB, start):
    here = 2 * pl.program_id(0)
    local = 2 * start + here
    q = first_ref[0] + local
    points = rhs_ref.shape[2]
    copies, blocks, _, part = grad_ref.shape
    cells = blocks * part

    @pl.when(pl.program_id(0) == 0)
    def _():
        for b in range(blocks):
            held[b] = functools.reduce(jnp.add, [grad_ref[copy, order_ref[b]] for copy in range(copies)])

    def latent(k, _):
        for b in range(blocks):
            row = held[b, pl.ds(local + k, 1), :]
            spread[b * part : (b + 1) * part, :] = jnp.broadcast_to(row, (128, part)).T
        totals = [jnp.zeros((8, 128), jnp.float32) for _ in range(points // 128)]
        for nb in range(cells // NB):
            rows = slice(nb * NB, (nb + 1) * NB)
            cell = lhs_ref[0, k, rows, :]
            e = jnp.exp2(jnp.dot(cell, rhs_ref[0], preferred_element_type=jnp.float32))
            grad = spread[rows, :]
            for c in range(points // 128):
                term = (e[:, c * 128 : (c + 1) * 128] * grad).reshape(NB // 8, 8, 128)
                totals[c] = totals[c] + jnp.sum(term, 0)
        row = jnp.concatenate([jnp.sum(total, 0, keepdims=True) for total in totals], 1)
        out_ref[pl.ds(here + k, 1), :] = row * var_ref[q + k]
        return 0

    for k in range(2):
        latent(k, 0)


def backward(first, order, var, grads, rhs, lhs, start, pairs):
    points = rhs.shape[2]
    _, blocks, own_q, part = grads.shape
    cells = blocks * part
    return pl.pallas_call(
        functools.partial(backward_kernel, NB=math.gcd(cells, 256), start=start),
        grid=(pairs,),
        out_shape=jax.ShapeDtypeStruct((2 * pairs, points), jnp.float32),
        in_specs=[whole(SMEM)] * 3
        + [
            whole(VMEM),
            pl.BlockSpec((1, 80, points), lambda i: (i + start, 0, 0)),
            pl.BlockSpec((1, 2, cells, 80), lambda i: (i + start, 0, 0, 0)),
        ],
        out_specs=whole(VMEM),
        scratch_shapes=[VMEM((blocks, own_q, part), jnp.float32), VMEM((cells, 128), jnp.float32)],
        compiler_params=pltpu.CompilerParams(vmem_limit_bytes=ROOM),
        cost_estimate=pl.CostEstimate(flops=25_000_000_000, bytes_accessed=4_000_000, transcendentals=0),
        name="backward",
    )(first, order, var, grads, *(pltpu.with_memory_space_constraint(x, pltpu.HBM) for x in (rhs, lhs)))


def gather_kernel(order_ref, *refs):
    *piece_refs, out_ref = refs
    each = len(piece_refs) // order_ref.shape[0]
    for step in range(order_ref.shape[0]):
        rows = jnp.concatenate([ref[...] for ref in piece_refs[step * each : (step + 1) * each]], 0)
        out_ref[order_ref[step]] = rows


def gather(order, pieces):
    count = order.shape[0]
    rows = sum(piece.shape[0] for piece in pieces) // count
    width = pieces[0].shape[1]
    out = pl.pallas_call(
        gather_kernel,
        out_shape=jax.ShapeDtypeStruct((count, rows, width), jnp.float32),
        in_specs=[whole(SMEM)] + [whole(VMEM)] * len(pieces),
        out_specs=whole(VMEM),
        compiler_params=pltpu.CompilerParams(vmem_limit_bytes=16 << 20),
        cost_estimate=pl.CostEstimate(flops=0, bytes_accessed=2_000_000, transcendentals=0),
        name="gather",
    )(order, *pieces)
    return out.reshape(count * rows, width)


def observe_kernel(index_ref, expr_hbm, out_hbm, expr_ref, out_ref, load_sem, store_sem):
    rows, genes = expr_ref.shape
    count, cells, width = out_ref.shape
    columns = [slice(j * width, (j + 1) * width) for j in range(genes // width)]
    loads = [
        pltpu.make_async_copy(expr_hbm.at[:, s], expr_ref.at[:, s], load_sem.at[j]) for j, s in enumerate(columns)
    ]
    for copy in loads:
        copy.start()
    places = lax.broadcasted_iota(jnp.int32, (cells, rows), 1)
    hot = jnp.where(places == index_ref[...], 1.0, 0.0).astype(jnp.bfloat16)
    stores = []
    for j, s in enumerate(columns):
        loads[j].wait()
        out_ref[j] = jnp.dot(hot, expr_ref[:, s], preferred_element_type=jnp.float32).astype(jnp.bfloat16)
        copy = pltpu.make_async_copy(out_ref.at[j], out_hbm.at[j], store_sem.at[j])
        copy.start()
        stores.append(copy)
    for copy in stores:
        copy.wait()


def observe(index, expr):
    rows, genes = expr.shape
    cells = index.shape[0]
    width = math.gcd(genes, 1024)
    count = genes // width
    return pl.pallas_call(
        observe_kernel,
        out_shape=pltpu.HBM((count, cells, width), jnp.bfloat16),
        in_specs=[whole(VMEM), whole(pltpu.HBM)],
        out_specs=whole(pltpu.HBM),
        scratch_shapes=[
            VMEM((rows, genes), jnp.bfloat16),
            VMEM((count, cells, width), jnp.bfloat16),
            pltpu.SemaphoreType.DMA((count,)),
            pltpu.SemaphoreType.DMA((count,)),
        ],
        compiler_params=pltpu.CompilerParams(vmem_limit_bytes=ROOM),
        cost_estimate=pl.CostEstimate(flops=3_000_000_000, bytes_accessed=6_000_000, transcendentals=0),
        name="observe",
    )(index[:, None], pltpu.with_memory_space_constraint(expr, pltpu.HBM))


def middle_kernel(rows_ref, piece_ref, mixing_ref, noise_ref, observed_ref, *rest, scale, cuts, shares):
    grad_refs, (send_ref, wide, latent) = rest[:shares], rest[shares:]
    latent_cuts, cell_cuts, lats, subs = cuts
    own_q, part = piece_ref.shape[2:]
    count, _, width = observed_ref.shape
    share = mixing_ref.shape[0] // shares
    for lat in range(lats):
        for a in range(latent_cuts):
            for b in range(cell_cuts):
                pieces = [piece_ref[a * cell_cuts + b, lat * subs + sub] for sub in range(subs)]
                first = (lat * latent_cuts + a) * own_q
                wide[first : first + own_q, b * part : (b + 1) * part] = functools.reduce(jnp.add, pieces)
    latent[...] = wide[...].astype(jnp.bfloat16)
    turned = wide[...].T.astype(jnp.bfloat16)
    halves = [latent[pl.ds(pl.multiple_of(rows_ref[i] * share, share), share), :] for i in range(shares)]
    ordered = jnp.concatenate(halves, 0)
    total = jnp.zeros(latent.shape, jnp.float32)
    for j in range(count):
        s = slice(j * width, (j + 1) * width)
        predicted = jnp.dot(turned, mixing_ref[:, s], preferred_element_type=jnp.float32)
        observed = observed_ref[j].astype(jnp.float32)
        weighted = (noise_ref[:, s] * (observed - predicted)).astype(jnp.bfloat16)
        grads = scale * jnp.dot(ordered, weighted, preferred_element_type=jnp.float32)
        for i in range(shares):
            grad_refs[i][:, s] = grads[i * share : (i + 1) * share]
        total = total + lax.dot_general(
            mixing_ref[:, s], weighted, (((1,), (1,)), ((), ())), preferred_element_type=jnp.float32
        )
    wide[...] = scale * total
    for lat in range(lats):
        for a in range(latent_cuts):
            for b in range(cell_cuts):
                first = (lat * latent_cuts + a) * own_q
                piece = wide[first : first + own_q, b * part : (b + 1) * part]
                for sub in range(subs):
                    send_ref[a * cell_cuts + b, lat * subs + sub] = piece


def middle(rows, pieces, mixing, noise, observed, scale, cuts):
    count, cells, width = observed.shape
    q, genes = mixing.shape
    shares = rows.shape[0]
    return pl.pallas_call(
        functools.partial(middle_kernel, scale=scale, cuts=cuts, shares=shares),
        out_shape=(jax.ShapeDtypeStruct((q // shares, genes), jnp.float32),) * shares
        + (jax.ShapeDtypeStruct(pieces.shape, jnp.float32),),
        in_specs=[whole(SMEM)] + [whole(VMEM)] * 4,
        out_specs=(whole(VMEM),) * (shares + 1),
        scratch_shapes=[
            VMEM((q, cells), jnp.float32),
            VMEM((q, cells), jnp.bfloat16),
        ],
        compiler_params=pltpu.CompilerParams(vmem_limit_bytes=ROOM),
        cost_estimate=pl.CostEstimate(flops=3_000_000_000, bytes_accessed=4_000_000, transcendentals=0),
        name="middle",
    )(
        rows,
        pieces,
        mixing,
        noise[None, :],
        pltpu.with_memory_space_constraint(observed, pltpu.HBM),
    )


def shifted(x, axes, step, size):
    return lax.ppermute(x, axes, [(partner(i, step, size), i) for i in range(size)])


def on_device(cell_index, coords_table, expr_table, inducing, ind_weights, lengthscale, variance, mixing, noise_prec):
    genes, lats, subs = (lax.axis_size(name) for name in ("gene", "lat", "sub"))
    blocks = lats * subs
    cells = cell_index.shape[0]
    local_q, points = ind_weights.shape
    latent_cuts = math.gcd(genes, local_q // 2)
    cell_cuts = genes // latent_cuts
    cuts = (latent_cuts, cell_cuts, lats, subs)
    own_q = local_q // latent_cuts
    part = cells // cell_cuts
    place = lax.axis_index("gene")
    block = lax.axis_index("lat") * subs + lax.axis_index("sub")
    first = (place // cell_cuts * own_q).reshape(1)
    order = jnp.stack([partner(block, step, blocks) for step in range(blocks)])
    every = ("gene", "lat", "sub")

    local_xy = locate(cell_index, coords_table)
    xys = [local_xy] + [shifted(local_xy, ("lat", "sub"), step, blocks) for step in range(1, blocks)]
    xys = [lax.dynamic_slice_in_dim(xy, place % cell_cuts * part, part, 1) for xy in xys]
    rhs = build(first, lengthscale, inducing, own_q)

    partial, lhs = forward(first, order, lengthscale, variance, ind_weights, rhs, xys, own_q, genes)
    late_index, partial = lax.optimization_barrier((cell_index, partial))
    pieces = lax.all_to_all(partial.reshape(genes * blocks, own_q, part), every, 0, 0, tiled=True)
    observed = observe(late_index, expr_table)

    grad_scale = -1.0 / math.sqrt(cells * blocks)
    sub = lax.axis_index("sub")
    rows = [sub ^ step if subs & (subs - 1) == 0 else (sub - step) % subs for step in range(subs)]
    *terms, send = middle(
        jnp.stack(rows), pieces.reshape(genes, blocks, own_q, part), mixing, noise_prec, observed, grad_scale, cuts
    )
    pieces = lax.all_to_all(send.reshape(genes * blocks, own_q, part), every, 0, 0, tiled=True)
    half = functools.reduce(
        jnp.add, [terms[0]] + [shifted(terms[step], "sub", step, subs) for step in range(1, subs)]
    )
    others = [shifted(half, "lat", step, lats) for step in range(1, lats)]

    grads = pieces.reshape(genes, blocks, own_q, part)
    pairs = own_q // 2
    early = pairs // 2 if cell_cuts == 1 else 0
    cut = [(0, early), (early, pairs)] if early else [(0, pairs)]
    inducing_terms, arrived = [], []
    for start, stop in cut:
        term = backward(first, order, variance, grads, rhs, lhs, start, stop - start)
        if start == 0:
            term, *others = lax.optimization_barrier((term, *others))
            half = functools.reduce(jnp.add, others, half)
        else:
            term, arrived = lax.optimization_barrier((term, arrived))
        inducing_terms.append(term)
        if cell_cuts == 1:
            arrived = arrived + [[shifted(term, "gene", step, genes) for step in range(1, genes)]]
    sub_order = jnp.stack([partner(sub, step, subs) for step in range(subs)])
    grad_mixing = gather(sub_order, [half] + [shifted(half, "sub", step, subs) for step in range(1, subs)])
    if cell_cuts == 1:
        gene_order = jnp.stack([partner(place, step, genes) for step in range(genes)])
        pieces = list(inducing_terms)
        for step in range(genes - 1):
            pieces += [parts[step] for parts in arrived]
        pieces, grad_mixing = lax.optimization_barrier((pieces, grad_mixing))
        return (grad_mixing, gather(gene_order, pieces))
    gathered = lax.all_gather(inducing_terms[0], "gene", axis=0, tiled=True)
    grad_inducing = gathered.reshape(latent_cuts, cell_cuts, own_q, points).sum(1)
    return (grad_mixing, grad_inducing.reshape(local_q, points))


def solution(mesh):
    in_specs = (
        P(("group", "lat", "sub")),
        P("group", ("lat", "sub")),
        P(("group", "lat", "sub"), "gene"),
        P("group", "lat", "sub"),
        P(("group", "lat"), "sub"),
        P(("group", "lat")),
        P(("group", "lat")),
        P("group", "gene"),
        P(("group", "gene")),
    )
    out_specs = (P("group", "gene"), P(("group", "lat"), "sub"))
    return jax.shard_map(
        on_device, mesh=mesh, in_specs=in_specs, out_specs=out_specs, check_vma=False
    )
```

```python
import functools
import math

import jax
import jax.numpy as jnp
from jax import lax
from jax.experimental import pallas as pl
from jax.experimental.pallas import tpu as pltpu
from jax.sharding import PartitionSpec as P

LOG2E = math.log2(math.e)
ROOM = 24 << 20

def row_of(shape):
    return lax.broadcasted_iota(jnp.int32, shape, 0)

def parts(u, w, a):
    L = u.shape[1]
    U = (u - 0.5) * a
    W = (w - 0.5) * a
    big = 1.5 * 2.0**20
    U1 = (U + big) - big
    W1 = (W + big) - big
    rU = U - U1
    rW = W - W1
    hi = U1 * U1 + W1 * W1
    lo = rU * (U1 + U) + rW * (W1 + W)
    r = row_of((8, L)) % 4
    T = jnp.where(r == 0, U, jnp.where(r == 1, W, jnp.where(r == 2, hi, lo)))
    rc = row_of((8, 1)) % 4
    magic = jnp.where(rc <= 1, 1.5 * 2.0**20, jnp.where(rc == 2, 1.5 * 2.0**26, 1.5 * 2.0**18)).astype(jnp.float32)
    T1 = ((T + magic) - magic).astype(jnp.bfloat16).astype(jnp.float32)
    R = T - T1
    T2 = R.astype(jnp.bfloat16).astype(jnp.float32)
    T3 = R - T2
    return T1, T2, T3

def point_rows(u, w, a):
    T1, T2, T3 = parts(u, w, a)
    return jnp.concatenate([T1, T2, T3, jnp.ones_like(T1)], 0).astype(jnp.bfloat16)


def spread_rows(rows):
    first, second = rows[:16], rows[16:]
    return jnp.concatenate([first, first, first, second, second], 0)

def cell_rows(u, w, a):
    T1, T2, T3 = parts(u, w, a)
    r8 = row_of(T1.shape)
    r = r8 % 4
    xy = r <= 1
    A1 = jnp.where(xy, 2 * T1, -1.0)
    A2 = jnp.where(xy, 2 * T2, 0.0)
    A3 = jnp.where(xy, 2 * T3, 0.0)
    outs = []
    for k in range(2):
        mine = (r8 // 4) == k
        G = [jnp.where(mine, A, 0.0) for A in (A1, A2, A3)]
        def n(T, i):
            return -T[4 * k + i : 4 * k + i + 1]
        z = jnp.zeros_like(n(T1, 0))
        norm = jnp.concatenate([n(T1, 2), n(T2, 2), n(T1, 3), n(T2, 3), n(T3, 3), z, z, z], 0)
        G1, G2, G3 = G
        outs.append(jnp.concatenate([G1, G1, G2, G2, G3, G3, G1, norm, G2, jnp.zeros_like(norm)], 0))
    return outs

VMEM = pltpu.VMEM
SMEM = pltpu.SMEM


def whole(space):
    return pl.BlockSpec(memory_space=space)


def partner(place, step, blocks):
    if blocks & (blocks - 1) == 0:
        return place ^ step
    return (place + step) % blocks


def locate_kernel(index_ref, table_ref, out_ref):
    table = table_ref[...]
    rows = table.shape[1]
    column = jnp.concatenate([table, jnp.zeros((8 - table.shape[0], rows), jnp.float32)], 0).T
    hot = lax.broadcasted_iota(jnp.int32, (rows, index_ref.shape[1]), 0) == index_ref[...]
    picked = [
        jnp.sum(jnp.where(hot, column[:, axis : axis + 1], 0.0), 0, keepdims=True)
        for axis in range(table.shape[0])
    ]
    out_ref[...] = jnp.concatenate(picked, 0)


def locate(index, table):
    return pl.pallas_call(
        locate_kernel,
        out_shape=jax.ShapeDtypeStruct((table.shape[0], index.shape[0]), jnp.float32),
        name="locate",
    )(index[None, :], table)


def scale_of(length_ref, q):
    lengths = jnp.where(row_of((8, 1)) < 4, length_ref[q], length_ref[q + 1])
    return math.sqrt(0.5 * LOG2E) / lengths


def build_kernel(first_ref, length_ref, points_ref, rhs_ref, *, aligned):
    local = 2 * pl.program_id(0)
    scale = scale_of(length_ref, first_ref[0] + local)
    row = local if aligned else first_ref[0] + local
    width = points_ref.shape[2]

    def step(i, _):
        s = pl.ds(pl.multiple_of(i * width, width), width)
        low = row_of((8, width)) < 4
        u, w = (
            jnp.where(low, points_ref[d, pl.ds(row, 1), s], points_ref[d, pl.ds(row + 1, 1), s]) for d in (0, 1)
        )
        rhs_ref[0, :, s] = point_rows(u, w, scale)
        return 0

    lax.fori_loop(0, points_ref.shape[2] // width, step, 0)


def build(first, lengths, points, own_q):
    axes, local_q, count = points.shape
    aligned = own_q % 8 == 0
    block = (axes, own_q if aligned else local_q, count)
    return pl.pallas_call(
        functools.partial(build_kernel, aligned=aligned),
        out_shape=pltpu.HBM((own_q // 2, 32, count), jnp.bfloat16),
        grid_spec=pltpu.PrefetchScalarGridSpec(
            num_scalar_prefetch=2,
            grid=(own_q // 2,),
            in_specs=[pl.BlockSpec(block, lambda i, first, _: (0, first[0] // own_q if aligned else 0, 0))],
            out_specs=pl.BlockSpec((1, 32, count), lambda i, *_: (i, 0, 0)),
        ),
        compiler_params=pltpu.CompilerParams(vmem_limit_bytes=16 << 20),
        cost_estimate=pl.CostEstimate(flops=4_000_000_000, bytes_accessed=4_000_000, transcendentals=0),
        name="build",
    )(first, pltpu.with_memory_space_constraint(lengths, pltpu.HBM), pltpu.with_memory_space_constraint(points, pltpu.HBM))


def forward_kernel(first_ref, order_ref, length_ref, var_ref, weight_ref, rhs_ref, *rest, blocks, NB, SB):
    xy_refs, (out_ref, lhs_ref, acc) = rest[:blocks], rest[blocks:]
    local = 2 * pl.program_id(0)
    q = first_ref[0] + local
    points = rhs_ref.shape[2]
    part = xy_refs[0].shape[1]
    cells = blocks * part
    scale = scale_of(length_ref, q)
    u, w = (
        jnp.broadcast_to(jnp.concatenate([ref[d : d + 1, :] for ref in xy_refs], 1), (8, cells)) for d in (0, 1)
    )
    for k, rows in enumerate(cell_rows(u, w, scale)):
        lhs_ref[0, k] = rows.T.astype(jnp.bfloat16)

    def latent(k, _):
        for nb in range(cells // NB):
            rows = slice(nb * NB, (nb + 1) * NB)
            cell = lhs_ref[0, k, rows, :]
            total = jnp.zeros((NB, 128), jnp.float32)
            for j in range(points // SB):
                s = slice(j * SB, (j + 1) * SB)
                e = jnp.exp2(jnp.dot(cell, spread_rows(rhs_ref[0, :, s]), preferred_element_type=jnp.float32))
                weight = weight_ref[pl.ds(q + k, 1), s]
                for c in range(SB // 128):
                    total = total + e[:, c * 128 : (c + 1) * 128] * weight[:, c * 128 : (c + 1) * 128]
            acc[rows, :] = total
        result = jnp.sum(acc[...].T, 0, keepdims=True) * var_ref[q + k]
        for b in range(blocks):
            for copy in range(out_ref.shape[0]):
                out_ref[copy, order_ref[b], pl.ds(local + k, 1), :] = result[:, b * part : (b + 1) * part]
        return 0

    for k in range(2):
        latent(k, 0)


def forward(first, order, lengths, var, weights, rhs, xys, own_q, copies):
    points = rhs.shape[2]
    blocks = len(xys)
    part = xys[0].shape[1]
    cells = blocks * part
    return pl.pallas_call(
        functools.partial(forward_kernel, blocks=blocks, NB=math.gcd(cells, 256), SB=points),
        grid=(own_q // 2,),
        out_shape=(
            jax.ShapeDtypeStruct((copies, blocks, own_q, part), jnp.float32),
            pltpu.HBM((own_q // 2, 2, cells, 80), jnp.bfloat16),
        ),
        in_specs=[whole(SMEM)] * 4
        + [whole(VMEM), pl.BlockSpec((1, 32, points), lambda i: (i, 0, 0))]
        + [whole(VMEM)] * blocks,
        out_specs=(whole(VMEM), pl.BlockSpec((1, 2, cells, 80), lambda i: (i, 0, 0, 0))),
        scratch_shapes=[VMEM((cells, 128), jnp.float32)],
        compiler_params=pltpu.CompilerParams(vmem_limit_bytes=ROOM),
        cost_estimate=pl.CostEstimate(flops=25_000_000_000, bytes_accessed=4_000_000, transcendentals=0),
        name="forward",
    )(first, order, lengths, var, weights, pltpu.with_memory_space_constraint(rhs, pltpu.HBM), *xys)


def backward_kernel(first_ref, order_ref, var_ref, grad_ref, rhs_ref, lhs_ref, out_ref, held, spread, *, NB, start):
    here = 2 * pl.program_id(0)
    local = 2 * start + here
    q = first_ref[0] + local
    points = rhs_ref.shape[2]
    copies, blocks, _, part = grad_ref.shape
    cells = blocks * part

    @pl.when(pl.program_id(0) == 0)
    def _():
        for b in range(blocks):
            held[b] = functools.reduce(jnp.add, [grad_ref[copy, order_ref[b]] for copy in range(copies)])

    def latent(k, _):
        for b in range(blocks):
            row = held[b, pl.ds(local + k, 1), :]
            spread[b * part : (b + 1) * part, :] = jnp.broadcast_to(row, (128, part)).T
        totals = [jnp.zeros((8, 128), jnp.float32) for _ in range(points // 128)]
        for nb in range(cells // NB):
            rows = slice(nb * NB, (nb + 1) * NB)
            cell = lhs_ref[0, k, rows, :]
            e = jnp.exp2(jnp.dot(cell, spread_rows(rhs_ref[0]), preferred_element_type=jnp.float32))
            grad = spread[rows, :]
            for c in range(points // 128):
                term = (e[:, c * 128 : (c + 1) * 128] * grad).reshape(NB // 8, 8, 128)
                totals[c] = totals[c] + jnp.sum(term, 0)
        row = jnp.concatenate([jnp.sum(total, 0, keepdims=True) for total in totals], 1)
        out_ref[pl.ds(here + k, 1), :] = row * var_ref[q + k]
        return 0

    for k in range(2):
        latent(k, 0)


def backward(first, order, var, grads, rhs, lhs, start, pairs):
    points = rhs.shape[2]
    _, blocks, own_q, part = grads.shape
    cells = blocks * part
    return pl.pallas_call(
        functools.partial(backward_kernel, NB=math.gcd(cells, 256), start=start),
        grid=(pairs,),
        out_shape=jax.ShapeDtypeStruct((2 * pairs, points), jnp.float32),
        in_specs=[whole(SMEM)] * 3
        + [
            whole(VMEM),
            pl.BlockSpec((1, 32, points), lambda i: (i + start, 0, 0)),
            pl.BlockSpec((1, 2, cells, 80), lambda i: (i + start, 0, 0, 0)),
        ],
        out_specs=whole(VMEM),
        scratch_shapes=[VMEM((blocks, own_q, part), jnp.float32), VMEM((cells, 128), jnp.float32)],
        compiler_params=pltpu.CompilerParams(vmem_limit_bytes=ROOM),
        cost_estimate=pl.CostEstimate(flops=25_000_000_000, bytes_accessed=4_000_000, transcendentals=0),
        name="backward",
    )(first, order, var, grads, *(pltpu.with_memory_space_constraint(x, pltpu.HBM) for x in (rhs, lhs)))


def gather_kernel(order_ref, *refs):
    *piece_refs, out_ref = refs
    each = len(piece_refs) // order_ref.shape[0]
    for step in range(order_ref.shape[0]):
        rows = jnp.concatenate([ref[...] for ref in piece_refs[step * each : (step + 1) * each]], 0)
        out_ref[order_ref[step]] = rows


def gather(order, pieces):
    count = order.shape[0]
    rows = sum(piece.shape[0] for piece in pieces) // count
    width = pieces[0].shape[1]
    out = pl.pallas_call(
        gather_kernel,
        out_shape=jax.ShapeDtypeStruct((count, rows, width), jnp.float32),
        in_specs=[whole(SMEM)] + [whole(VMEM)] * len(pieces),
        out_specs=whole(VMEM),
        compiler_params=pltpu.CompilerParams(vmem_limit_bytes=16 << 20),
        cost_estimate=pl.CostEstimate(flops=0, bytes_accessed=2_000_000, transcendentals=0),
        name="gather",
    )(order, *pieces)
    return out.reshape(count * rows, width)


def observe_kernel(index_ref, expr_hbm, out_hbm, expr_ref, out_ref, load_sem, store_sem):
    rows, genes = expr_ref.shape
    count, cells, width = out_ref.shape
    columns = [slice(j * width, (j + 1) * width) for j in range(genes // width)]
    loads = [
        pltpu.make_async_copy(expr_hbm.at[:, s], expr_ref.at[:, s], load_sem.at[j]) for j, s in enumerate(columns)
    ]
    for copy in loads:
        copy.start()
    places = lax.broadcasted_iota(jnp.int32, (cells, rows), 1)
    hot = jnp.where(places == index_ref[...], 1.0, 0.0).astype(jnp.bfloat16)
    stores = []
    for j, s in enumerate(columns):
        loads[j].wait()
        out_ref[j] = jnp.dot(hot, expr_ref[:, s], preferred_element_type=jnp.float32).astype(jnp.bfloat16)
        copy = pltpu.make_async_copy(out_ref.at[j], out_hbm.at[j], store_sem.at[j])
        copy.start()
        stores.append(copy)
    for copy in stores:
        copy.wait()


def observe(index, expr):
    rows, genes = expr.shape
    cells = index.shape[0]
    width = math.gcd(genes, 1024)
    count = genes // width
    return pl.pallas_call(
        observe_kernel,
        out_shape=pltpu.HBM((count, cells, width), jnp.bfloat16),
        in_specs=[whole(VMEM), whole(pltpu.HBM)],
        out_specs=whole(pltpu.HBM),
        scratch_shapes=[
            VMEM((rows, genes), jnp.bfloat16),
            VMEM((count, cells, width), jnp.bfloat16),
            pltpu.SemaphoreType.DMA((count,)),
            pltpu.SemaphoreType.DMA((count,)),
        ],
        compiler_params=pltpu.CompilerParams(vmem_limit_bytes=ROOM),
        cost_estimate=pl.CostEstimate(flops=3_000_000_000, bytes_accessed=6_000_000, transcendentals=0),
        name="observe",
    )(index[:, None], pltpu.with_memory_space_constraint(expr, pltpu.HBM))


def middle_kernel(rows_ref, piece_ref, mixing_ref, noise_ref, observed_ref, *rest, scale, cuts, shares):
    grad_refs, (send_ref, wide, latent) = rest[:shares], rest[shares:]
    latent_cuts, cell_cuts, lats, subs = cuts
    own_q, part = piece_ref.shape[2:]
    count, _, width = observed_ref.shape
    share = mixing_ref.shape[0] // shares
    for lat in range(lats):
        for a in range(latent_cuts):
            for b in range(cell_cuts):
                pieces = [piece_ref[a * cell_cuts + b, lat * subs + sub] for sub in range(subs)]
                first = (lat * latent_cuts + a) * own_q
                wide[first : first + own_q, b * part : (b + 1) * part] = functools.reduce(jnp.add, pieces)
    latent[...] = wide[...].astype(jnp.bfloat16)
    turned = wide[...].T.astype(jnp.bfloat16)
    halves = [latent[pl.ds(pl.multiple_of(rows_ref[i] * share, share), share), :] for i in range(shares)]
    ordered = jnp.concatenate(halves, 0)
    total = jnp.zeros(latent.shape, jnp.float32)
    for j in range(count):
        s = slice(j * width, (j + 1) * width)
        predicted = jnp.dot(turned, mixing_ref[:, s], preferred_element_type=jnp.float32)
        observed = observed_ref[j].astype(jnp.float32)
        weighted = (noise_ref[:, s] * (observed - predicted)).astype(jnp.bfloat16)
        grads = scale * jnp.dot(ordered, weighted, preferred_element_type=jnp.float32)
        for i in range(shares):
            grad_refs[i][:, s] = grads[i * share : (i + 1) * share]
        total = total + lax.dot_general(
            mixing_ref[:, s], weighted, (((1,), (1,)), ((), ())), preferred_element_type=jnp.float32
        )
    wide[...] = scale * total
    for lat in range(lats):
        for a in range(latent_cuts):
            for b in range(cell_cuts):
                first = (lat * latent_cuts + a) * own_q
                piece = wide[first : first + own_q, b * part : (b + 1) * part]
                for sub in range(subs):
                    send_ref[a * cell_cuts + b, lat * subs + sub] = piece


def middle(rows, pieces, mixing, noise, observed, scale, cuts):
    count, cells, width = observed.shape
    q, genes = mixing.shape
    shares = rows.shape[0]
    return pl.pallas_call(
        functools.partial(middle_kernel, scale=scale, cuts=cuts, shares=shares),
        out_shape=(jax.ShapeDtypeStruct((q // shares, genes), jnp.float32),) * shares
        + (jax.ShapeDtypeStruct(pieces.shape, jnp.float32),),
        in_specs=[whole(SMEM)] + [whole(VMEM)] * 4,
        out_specs=(whole(VMEM),) * (shares + 1),
        scratch_shapes=[
            VMEM((q, cells), jnp.float32),
            VMEM((q, cells), jnp.bfloat16),
        ],
        compiler_params=pltpu.CompilerParams(vmem_limit_bytes=ROOM),
        cost_estimate=pl.CostEstimate(flops=3_000_000_000, bytes_accessed=4_000_000, transcendentals=0),
        name="middle",
    )(
        rows,
        pieces,
        mixing,
        noise[None, :],
        pltpu.with_memory_space_constraint(observed, pltpu.HBM),
    )


def shifted(x, axes, step, size):
    return lax.ppermute(x, axes, [(partner(i, step, size), i) for i in range(size)])


def on_device(cell_index, coords_table, expr_table, inducing, ind_weights, lengthscale, variance, mixing, noise_prec):
    genes, lats, subs = (lax.axis_size(name) for name in ("gene", "lat", "sub"))
    blocks = lats * subs
    cells = cell_index.shape[0]
    local_q, points = ind_weights.shape
    latent_cuts = math.gcd(genes, local_q // 2)
    cell_cuts = genes // latent_cuts
    cuts = (latent_cuts, cell_cuts, lats, subs)
    own_q = local_q // latent_cuts
    part = cells // cell_cuts
    place = lax.axis_index("gene")
    block = lax.axis_index("lat") * subs + lax.axis_index("sub")
    first = (place // cell_cuts * own_q).reshape(1)
    order = jnp.stack([partner(block, step, blocks) for step in range(blocks)])
    every = ("gene", "lat", "sub")

    local_xy = locate(cell_index, coords_table)
    xys = [local_xy] + [shifted(local_xy, ("lat", "sub"), step, blocks) for step in range(1, blocks)]
    xys = [lax.dynamic_slice_in_dim(xy, place % cell_cuts * part, part, 1) for xy in xys]
    rhs = build(first, lengthscale, inducing, own_q)

    partial, lhs = forward(first, order, lengthscale, variance, ind_weights, rhs, xys, own_q, genes)
    late_index, partial = lax.optimization_barrier((cell_index, partial))
    pieces = lax.all_to_all(partial.reshape(genes * blocks, own_q, part), every, 0, 0, tiled=True)
    observed = observe(late_index, expr_table)

    grad_scale = -1.0 / math.sqrt(cells * blocks)
    sub = lax.axis_index("sub")
    rows = [sub ^ step if subs & (subs - 1) == 0 else (sub - step) % subs for step in range(subs)]
    *terms, send = middle(
        jnp.stack(rows), pieces.reshape(genes, blocks, own_q, part), mixing, noise_prec, observed, grad_scale, cuts
    )
    pieces = lax.all_to_all(send.reshape(genes * blocks, own_q, part), every, 0, 0, tiled=True)
    half = functools.reduce(
        jnp.add, [terms[0]] + [shifted(terms[step], "sub", step, subs) for step in range(1, subs)]
    )
    others = [shifted(half, "lat", step, lats) for step in range(1, lats)]

    grads = pieces.reshape(genes, blocks, own_q, part)
    pairs = own_q // 2
    early = pairs // 2 if cell_cuts == 1 else 0
    cut = [(0, early), (early, pairs)] if early else [(0, pairs)]
    inducing_terms, arrived = [], []
    for start, stop in cut:
        term = backward(first, order, variance, grads, rhs, lhs, start, stop - start)
        if start == 0:
            term, *others = lax.optimization_barrier((term, *others))
            half = functools.reduce(jnp.add, others, half)
        else:
            term, arrived = lax.optimization_barrier((term, arrived))
        inducing_terms.append(term)
        if cell_cuts == 1:
            arrived = arrived + [[shifted(term, "gene", step, genes) for step in range(1, genes)]]
    sub_order = jnp.stack([partner(sub, step, subs) for step in range(subs)])
    grad_mixing = gather(sub_order, [half] + [shifted(half, "sub", step, subs) for step in range(1, subs)])
    if cell_cuts == 1:
        gene_order = jnp.stack([partner(place, step, genes) for step in range(genes)])
        pieces = list(inducing_terms)
        for step in range(genes - 1):
            pieces += [parts[step] for parts in arrived]
        pieces, grad_mixing = lax.optimization_barrier((pieces, grad_mixing))
        return (grad_mixing, gather(gene_order, pieces))
    gathered = lax.all_gather(inducing_terms[0], "gene", axis=0, tiled=True)
    grad_inducing = gathered.reshape(latent_cuts, cell_cuts, own_q, points).sum(1)
    return (grad_mixing, grad_inducing.reshape(local_q, points))


def solution(mesh):
    in_specs = (
        P(("group", "lat", "sub")),
        P("group", ("lat", "sub")),
        P(("group", "lat", "sub"), "gene"),
        P("group", "lat", "sub"),
        P(("group", "lat"), "sub"),
        P(("group", "lat")),
        P(("group", "lat")),
        P("group", "gene"),
        P(("group", "gene")),
    )
    out_specs = (P("group", "gene"), P(("group", "lat"), "sub"))
    return jax.shard_map(
        on_device, mesh=mesh, in_specs=in_specs, out_specs=out_specs, check_vma=False
    )
```

```python
import functools
import math

import jax
import jax.numpy as jnp
from jax import lax
from jax.experimental import pallas as pl
from jax.experimental.pallas import tpu as pltpu
from jax.sharding import PartitionSpec as P

LOG2E = math.log2(math.e)
ROOM = 24 << 20

def row_of(shape):
    return lax.broadcasted_iota(jnp.int32, shape, 0)

def parts(u, w, a):
    L = u.shape[1]
    U = (u - 0.5) * a
    W = (w - 0.5) * a
    big = 1.5 * 2.0**20
    U1 = (U + big) - big
    W1 = (W + big) - big
    rU = U - U1
    rW = W - W1
    hi = U1 * U1 + W1 * W1
    lo = rU * (U1 + U) + rW * (W1 + W)
    r = row_of((8, L)) % 4
    T = jnp.where(r == 0, U, jnp.where(r == 1, W, jnp.where(r == 2, hi, lo)))
    rc = row_of((8, 1)) % 4
    magic = jnp.where(rc <= 1, 1.5 * 2.0**20, jnp.where(rc == 2, 1.5 * 2.0**26, 1.5 * 2.0**18)).astype(jnp.float32)
    T1 = ((T + magic) - magic).astype(jnp.bfloat16).astype(jnp.float32)
    R = T - T1
    T2 = R.astype(jnp.bfloat16).astype(jnp.float32)
    T3 = R - T2
    return T1, T2, T3

def point_rows(u, w, a):
    T1, T2, T3 = parts(u, w, a)
    return jnp.concatenate([T1, T2, T3, jnp.ones_like(T1)], 0).astype(jnp.bfloat16)


def spread_rows(rows):
    first, second = rows[:16], rows[16:]
    return jnp.concatenate([first, first, first, second, second], 0)

def cell_rows(u, w, a):
    T1, T2, T3 = parts(u, w, a)
    r8 = row_of(T1.shape)
    r = r8 % 4
    xy = r <= 1
    A1 = jnp.where(xy, 2 * T1, -1.0)
    A2 = jnp.where(xy, 2 * T2, 0.0)
    A3 = jnp.where(xy, 2 * T3, 0.0)
    outs = []
    for k in range(2):
        mine = (r8 // 4) == k
        G = [jnp.where(mine, A, 0.0) for A in (A1, A2, A3)]
        def n(T, i):
            return -T[4 * k + i : 4 * k + i + 1]
        z = jnp.zeros_like(n(T1, 0))
        norm = jnp.concatenate([n(T1, 2), n(T2, 2), n(T1, 3), n(T2, 3), n(T3, 3), z, z, z], 0)
        G1, G2, G3 = G
        outs.append(jnp.concatenate([G1, G1, G2, G2, G3, G3, G1, norm, G2, jnp.zeros_like(norm)], 0))
    return outs

VMEM = pltpu.VMEM
SMEM = pltpu.SMEM


def whole(space):
    return pl.BlockSpec(memory_space=space)


def partner(place, step, blocks):
    if blocks & (blocks - 1) == 0:
        return place ^ step
    return (place + step) % blocks


def locate_kernel(index_ref, table_ref, out_ref):
    table = table_ref[...]
    rows = table.shape[1]
    column = jnp.concatenate([table, jnp.zeros((8 - table.shape[0], rows), jnp.float32)], 0).T
    hot = lax.broadcasted_iota(jnp.int32, (rows, index_ref.shape[1]), 0) == index_ref[...]
    picked = [
        jnp.sum(jnp.where(hot, column[:, axis : axis + 1], 0.0), 0, keepdims=True)
        for axis in range(table.shape[0])
    ]
    out_ref[...] = jnp.concatenate(picked, 0)


def locate(index, table):
    return pl.pallas_call(
        locate_kernel,
        out_shape=jax.ShapeDtypeStruct((table.shape[0], index.shape[0]), jnp.float32),
        name="locate",
    )(index[None, :], table)


def scale_of(length_ref, q):
    lengths = jnp.where(row_of((8, 1)) < 4, length_ref[q], length_ref[q + 1])
    return math.sqrt(0.5 * LOG2E) / lengths


def build_kernel(first_ref, length_ref, points_ref, rhs_ref, *, aligned):
    low = row_of((8, points_ref.shape[2])) < 4
    for pair in range(rhs_ref.shape[0]):
        local = 2 * pair
        scale = scale_of(length_ref, first_ref[0] + local)
        row = local if aligned else first_ref[0] + local
        u, w = (
            jnp.where(low, points_ref[d, pl.ds(row, 1), :], points_ref[d, pl.ds(row + 1, 1), :]) for d in (0, 1)
        )
        rhs_ref[pair] = point_rows(u, w, scale)


def build(first, lengths, points, own_q):
    axes, local_q, count = points.shape
    aligned = own_q % 8 == 0
    block = (axes, own_q if aligned else local_q, count)
    return pl.pallas_call(
        functools.partial(build_kernel, aligned=aligned),
        out_shape=pltpu.HBM((own_q // 2, 32, count), jnp.bfloat16),
        grid_spec=pltpu.PrefetchScalarGridSpec(
            num_scalar_prefetch=2,
            grid=(1,),
            in_specs=[pl.BlockSpec(block, lambda i, first, _: (0, first[0] // own_q if aligned else 0, 0))],
            out_specs=pl.BlockSpec((own_q // 2, 32, count), lambda i, *_: (0, 0, 0)),
        ),
        compiler_params=pltpu.CompilerParams(vmem_limit_bytes=16 << 20),
        cost_estimate=pl.CostEstimate(flops=4_000_000_000, bytes_accessed=4_000_000, transcendentals=0),
        name="build",
    )(first, pltpu.with_memory_space_constraint(lengths, pltpu.HBM), pltpu.with_memory_space_constraint(points, pltpu.HBM))


def forward_kernel(first_ref, order_ref, length_ref, var_ref, weight_ref, rhs_ref, *rest, blocks, NB, SB):
    xy_refs, (out_ref, lhs_ref, acc) = rest[:blocks], rest[blocks:]
    local = 2 * pl.program_id(0)
    q = first_ref[0] + local
    points = rhs_ref.shape[2]
    part = xy_refs[0].shape[1]
    cells = blocks * part
    scale = scale_of(length_ref, q)
    u, w = (
        jnp.broadcast_to(jnp.concatenate([ref[d : d + 1, :] for ref in xy_refs], 1), (8, cells)) for d in (0, 1)
    )
    for k, rows in enumerate(cell_rows(u, w, scale)):
        lhs_ref[0, k] = rows.T.astype(jnp.bfloat16)

    def latent(k, _):
        for nb in range(cells // NB):
            rows = slice(nb * NB, (nb + 1) * NB)
            cell = lhs_ref[0, k, rows, :]
            total = jnp.zeros((NB, 128), jnp.float32)
            for j in range(points // SB):
                s = slice(j * SB, (j + 1) * SB)
                e = jnp.exp2(jnp.dot(cell, spread_rows(rhs_ref[0, :, s]), preferred_element_type=jnp.float32))
                weight = weight_ref[pl.ds(q + k, 1), s]
                for c in range(SB // 128):
                    total = total + e[:, c * 128 : (c + 1) * 128] * weight[:, c * 128 : (c + 1) * 128]
            acc[rows, :] = total
        result = jnp.sum(acc[...].T, 0, keepdims=True) * var_ref[q + k]
        for b in range(blocks):
            for copy in range(out_ref.shape[0]):
                out_ref[copy, order_ref[b], pl.ds(local + k, 1), :] = result[:, b * part : (b + 1) * part]
        return 0

    for k in range(2):
        latent(k, 0)


def forward(first, order, lengths, var, weights, rhs, xys, own_q, copies):
    points = rhs.shape[2]
    blocks = len(xys)
    part = xys[0].shape[1]
    cells = blocks * part
    return pl.pallas_call(
        functools.partial(forward_kernel, blocks=blocks, NB=math.gcd(cells, 256), SB=points),
        grid=(own_q // 2,),
        out_shape=(
            jax.ShapeDtypeStruct((copies, blocks, own_q, part), jnp.float32),
            pltpu.HBM((own_q // 2, 2, cells, 80), jnp.bfloat16),
        ),
        in_specs=[whole(SMEM)] * 4
        + [whole(VMEM), pl.BlockSpec((1, 32, points), lambda i: (i, 0, 0))]
        + [whole(VMEM)] * blocks,
        out_specs=(whole(VMEM), pl.BlockSpec((1, 2, cells, 80), lambda i: (i, 0, 0, 0))),
        scratch_shapes=[VMEM((cells, 128), jnp.float32)],
        compiler_params=pltpu.CompilerParams(vmem_limit_bytes=ROOM),
        cost_estimate=pl.CostEstimate(flops=25_000_000_000, bytes_accessed=4_000_000, transcendentals=0),
        name="forward",
    )(first, order, lengths, var, weights, pltpu.with_memory_space_constraint(rhs, pltpu.HBM), *xys)


def backward_kernel(first_ref, order_ref, var_ref, grad_ref, rhs_ref, lhs_ref, out_ref, held, spread, *, NB, start):
    here = 2 * pl.program_id(0)
    local = 2 * start + here
    q = first_ref[0] + local
    points = rhs_ref.shape[2]
    copies, blocks, _, part = grad_ref.shape
    cells = blocks * part

    @pl.when(pl.program_id(0) == 0)
    def _():
        for b in range(blocks):
            held[b] = functools.reduce(jnp.add, [grad_ref[copy, order_ref[b]] for copy in range(copies)])

    def latent(k, _):
        for b in range(blocks):
            row = held[b, pl.ds(local + k, 1), :]
            spread[b * part : (b + 1) * part, :] = jnp.broadcast_to(row, (128, part)).T
        totals = [jnp.zeros((8, 128), jnp.float32) for _ in range(points // 128)]
        for nb in range(cells // NB):
            rows = slice(nb * NB, (nb + 1) * NB)
            cell = lhs_ref[0, k, rows, :]
            e = jnp.exp2(jnp.dot(cell, spread_rows(rhs_ref[0]), preferred_element_type=jnp.float32))
            grad = spread[rows, :]
            for c in range(points // 128):
                term = (e[:, c * 128 : (c + 1) * 128] * grad).reshape(NB // 8, 8, 128)
                totals[c] = totals[c] + jnp.sum(term, 0)
        row = jnp.concatenate([jnp.sum(total, 0, keepdims=True) for total in totals], 1)
        out_ref[pl.ds(here + k, 1), :] = row * var_ref[q + k]
        return 0

    for k in range(2):
        latent(k, 0)


def backward(first, order, var, grads, rhs, lhs, start, pairs):
    points = rhs.shape[2]
    _, blocks, own_q, part = grads.shape
    cells = blocks * part
    return pl.pallas_call(
        functools.partial(backward_kernel, NB=math.gcd(cells, 256), start=start),
        grid=(pairs,),
        out_shape=jax.ShapeDtypeStruct((2 * pairs, points), jnp.float32),
        in_specs=[whole(SMEM)] * 3
        + [
            whole(VMEM),
            pl.BlockSpec((1, 32, points), lambda i: (i + start, 0, 0)),
            pl.BlockSpec((1, 2, cells, 80), lambda i: (i + start, 0, 0, 0)),
        ],
        out_specs=whole(VMEM),
        scratch_shapes=[VMEM((blocks, own_q, part), jnp.float32), VMEM((cells, 128), jnp.float32)],
        compiler_params=pltpu.CompilerParams(vmem_limit_bytes=ROOM),
        cost_estimate=pl.CostEstimate(flops=25_000_000_000, bytes_accessed=4_000_000, transcendentals=0),
        name="backward",
    )(first, order, var, grads, *(pltpu.with_memory_space_constraint(x, pltpu.HBM) for x in (rhs, lhs)))


def gather_kernel(order_ref, *refs):
    *piece_refs, out_ref = refs
    each = len(piece_refs) // order_ref.shape[0]
    for step in range(order_ref.shape[0]):
        rows = jnp.concatenate([ref[...] for ref in piece_refs[step * each : (step + 1) * each]], 0)
        out_ref[order_ref[step]] = rows


def gather(order, pieces):
    count = order.shape[0]
    rows = sum(piece.shape[0] for piece in pieces) // count
    width = pieces[0].shape[1]
    out = pl.pallas_call(
        gather_kernel,
        out_shape=jax.ShapeDtypeStruct((count, rows, width), jnp.float32),
        in_specs=[whole(SMEM)] + [whole(VMEM)] * len(pieces),
        out_specs=whole(VMEM),
        compiler_params=pltpu.CompilerParams(vmem_limit_bytes=16 << 20),
        cost_estimate=pl.CostEstimate(flops=0, bytes_accessed=2_000_000, transcendentals=0),
        name="gather",
    )(order, *pieces)
    return out.reshape(count * rows, width)


def observe_kernel(index_ref, expr_hbm, out_hbm, expr_ref, out_ref, load_sem, store_sem):
    rows, genes = expr_ref.shape
    count, cells, width = out_ref.shape
    columns = [slice(j * width, (j + 1) * width) for j in range(genes // width)]
    loads = [
        pltpu.make_async_copy(expr_hbm.at[:, s], expr_ref.at[:, s], load_sem.at[j]) for j, s in enumerate(columns)
    ]
    for copy in loads:
        copy.start()
    places = lax.broadcasted_iota(jnp.int32, (cells, rows), 1)
    hot = jnp.where(places == index_ref[...], 1.0, 0.0).astype(jnp.bfloat16)
    stores = []
    for j, s in enumerate(columns):
        loads[j].wait()
        out_ref[j] = jnp.dot(hot, expr_ref[:, s], preferred_element_type=jnp.float32).astype(jnp.bfloat16)
        copy = pltpu.make_async_copy(out_ref.at[j], out_hbm.at[j], store_sem.at[j])
        copy.start()
        stores.append(copy)
    for copy in stores:
        copy.wait()


def observe(index, expr):
    rows, genes = expr.shape
    cells = index.shape[0]
    width = math.gcd(genes, 1024)
    count = genes // width
    return pl.pallas_call(
        observe_kernel,
        out_shape=pltpu.HBM((count, cells, width), jnp.bfloat16),
        in_specs=[whole(VMEM), whole(pltpu.HBM)],
        out_specs=whole(pltpu.HBM),
        scratch_shapes=[
            VMEM((rows, genes), jnp.bfloat16),
            VMEM((count, cells, width), jnp.bfloat16),
            pltpu.SemaphoreType.DMA((count,)),
            pltpu.SemaphoreType.DMA((count,)),
        ],
        compiler_params=pltpu.CompilerParams(vmem_limit_bytes=ROOM),
        cost_estimate=pl.CostEstimate(flops=3_000_000_000, bytes_accessed=6_000_000, transcendentals=0),
        name="observe",
    )(index[:, None], pltpu.with_memory_space_constraint(expr, pltpu.HBM))


def middle_kernel(rows_ref, piece_ref, mixing_ref, noise_ref, observed_ref, *rest, scale, cuts, shares):
    grad_refs, (send_ref, wide, latent) = rest[:shares], rest[shares:]
    latent_cuts, cell_cuts, lats, subs = cuts
    own_q, part = piece_ref.shape[2:]
    count, _, width = observed_ref.shape
    share = mixing_ref.shape[0] // shares
    for lat in range(lats):
        for a in range(latent_cuts):
            for b in range(cell_cuts):
                pieces = [piece_ref[a * cell_cuts + b, lat * subs + sub] for sub in range(subs)]
                first = (lat * latent_cuts + a) * own_q
                wide[first : first + own_q, b * part : (b + 1) * part] = functools.reduce(jnp.add, pieces)
    latent[...] = wide[...].astype(jnp.bfloat16)
    turned = wide[...].T.astype(jnp.bfloat16)
    halves = [latent[pl.ds(pl.multiple_of(rows_ref[i] * share, share), share), :] for i in range(shares)]
    ordered = jnp.concatenate(halves, 0)
    total = jnp.zeros(latent.shape, jnp.float32)
    for j in range(count):
        s = slice(j * width, (j + 1) * width)
        predicted = jnp.dot(turned, mixing_ref[:, s], preferred_element_type=jnp.float32)
        observed = observed_ref[j].astype(jnp.float32)
        weighted = (noise_ref[:, s] * (observed - predicted)).astype(jnp.bfloat16)
        grads = scale * jnp.dot(ordered, weighted, preferred_element_type=jnp.float32)
        for i in range(shares):
            grad_refs[i][:, s] = grads[i * share : (i + 1) * share]
        total = total + lax.dot_general(
            mixing_ref[:, s], weighted, (((1,), (1,)), ((), ())), preferred_element_type=jnp.float32
        )
    wide[...] = scale * total
    for lat in range(lats):
        for a in range(latent_cuts):
            for b in range(cell_cuts):
                first = (lat * latent_cuts + a) * own_q
                piece = wide[first : first + own_q, b * part : (b + 1) * part]
                for sub in range(subs):
                    send_ref[a * cell_cuts + b, lat * subs + sub] = piece


def middle(rows, pieces, mixing, noise, observed, scale, cuts):
    count, cells, width = observed.shape
    q, genes = mixing.shape
    shares = rows.shape[0]
    return pl.pallas_call(
        functools.partial(middle_kernel, scale=scale, cuts=cuts, shares=shares),
        out_shape=(jax.ShapeDtypeStruct((q // shares, genes), jnp.float32),) * shares
        + (jax.ShapeDtypeStruct(pieces.shape, jnp.float32),),
        in_specs=[whole(SMEM)] + [whole(VMEM)] * 4,
        out_specs=(whole(VMEM),) * (shares + 1),
        scratch_shapes=[
            VMEM((q, cells), jnp.float32),
            VMEM((q, cells), jnp.bfloat16),
        ],
        compiler_params=pltpu.CompilerParams(vmem_limit_bytes=ROOM),
        cost_estimate=pl.CostEstimate(flops=3_000_000_000, bytes_accessed=4_000_000, transcendentals=0),
        name="middle",
    )(
        rows,
        pieces,
        mixing,
        noise[None, :],
        pltpu.with_memory_space_constraint(observed, pltpu.HBM),
    )


def shifted(x, axes, step, size):
    return lax.ppermute(x, axes, [(partner(i, step, size), i) for i in range(size)])


def on_device(cell_index, coords_table, expr_table, inducing, ind_weights, lengthscale, variance, mixing, noise_prec):
    genes, lats, subs = (lax.axis_size(name) for name in ("gene", "lat", "sub"))
    blocks = lats * subs
    cells = cell_index.shape[0]
    local_q, points = ind_weights.shape
    latent_cuts = math.gcd(genes, local_q // 2)
    cell_cuts = genes // latent_cuts
    cuts = (latent_cuts, cell_cuts, lats, subs)
    own_q = local_q // latent_cuts
    part = cells // cell_cuts
    place = lax.axis_index("gene")
    block = lax.axis_index("lat") * subs + lax.axis_index("sub")
    first = (place // cell_cuts * own_q).reshape(1)
    order = jnp.stack([partner(block, step, blocks) for step in range(blocks)])
    every = ("gene", "lat", "sub")

    local_xy = locate(cell_index, coords_table)
    xys = [local_xy] + [shifted(local_xy, ("lat", "sub"), step, blocks) for step in range(1, blocks)]
    xys = [lax.dynamic_slice_in_dim(xy, place % cell_cuts * part, part, 1) for xy in xys]
    rhs = build(first, lengthscale, inducing, own_q)

    partial, lhs = forward(first, order, lengthscale, variance, ind_weights, rhs, xys, own_q, genes)
    late_index, partial = lax.optimization_barrier((cell_index, partial))
    pieces = lax.all_to_all(partial.reshape(genes * blocks, own_q, part), every, 0, 0, tiled=True)
    observed = observe(late_index, expr_table)

    grad_scale = -1.0 / math.sqrt(cells * blocks)
    sub = lax.axis_index("sub")
    rows = [sub ^ step if subs & (subs - 1) == 0 else (sub - step) % subs for step in range(subs)]
    *terms, send = middle(
        jnp.stack(rows), pieces.reshape(genes, blocks, own_q, part), mixing, noise_prec, observed, grad_scale, cuts
    )
    pieces = lax.all_to_all(send.reshape(genes * blocks, own_q, part), every, 0, 0, tiled=True)
    half = functools.reduce(
        jnp.add, [terms[0]] + [shifted(terms[step], "sub", step, subs) for step in range(1, subs)]
    )
    others = [shifted(half, "lat", step, lats) for step in range(1, lats)]

    grads = pieces.reshape(genes, blocks, own_q, part)
    pairs = own_q // 2
    early = pairs // 2 if cell_cuts == 1 else 0
    cut = [(0, early), (early, pairs)] if early else [(0, pairs)]
    inducing_terms, arrived = [], []
    for start, stop in cut:
        term = backward(first, order, variance, grads, rhs, lhs, start, stop - start)
        if start == 0:
            term, *others = lax.optimization_barrier((term, *others))
            half = functools.reduce(jnp.add, others, half)
        else:
            term, arrived = lax.optimization_barrier((term, arrived))
        inducing_terms.append(term)
        if cell_cuts == 1:
            arrived = arrived + [[shifted(term, "gene", step, genes) for step in range(1, genes)]]
    sub_order = jnp.stack([partner(sub, step, subs) for step in range(subs)])
    grad_mixing = gather(sub_order, [half] + [shifted(half, "sub", step, subs) for step in range(1, subs)])
    if cell_cuts == 1:
        gene_order = jnp.stack([partner(place, step, genes) for step in range(genes)])
        pieces = list(inducing_terms)
        for step in range(genes - 1):
            pieces += [parts[step] for parts in arrived]
        pieces, grad_mixing = lax.optimization_barrier((pieces, grad_mixing))
        return (grad_mixing, gather(gene_order, pieces))
    gathered = lax.all_gather(inducing_terms[0], "gene", axis=0, tiled=True)
    grad_inducing = gathered.reshape(latent_cuts, cell_cuts, own_q, points).sum(1)
    return (grad_mixing, grad_inducing.reshape(local_q, points))


def solution(mesh):
    in_specs = (
        P(("group", "lat", "sub")),
        P("group", ("lat", "sub")),
        P(("group", "lat", "sub"), "gene"),
        P("group", "lat", "sub"),
        P(("group", "lat"), "sub"),
        P(("group", "lat")),
        P(("group", "lat")),
        P("group", "gene"),
        P(("group", "gene")),
    )
    out_specs = (P("group", "gene"), P(("group", "lat"), "sub"))
    return jax.shard_map(
        on_device, mesh=mesh, in_specs=in_specs, out_specs=out_specs, check_vma=False
    )
```
